128 devices in a mesh: row: 8 (over y, core), col: 16 (over z, x).
Axes of the slice: x: 4, y: 4, z: 4, core: 2. Of those that a mesh axis runs over, the one named last changes fastest.
Arguments:
- weights: bfloat16 [8192, 8192], P('row', 'col')
- panel: bfloat16 [8192, 8192], P('row', 'col'), may hold values from 0.0099487305 to 1
- pattern: int32 [32, 32], P('row', 'col'), may hold values from 0 to 1, as said below
Outputs:
- flow: float32 [8192, 8192], P('row', 'col')
The draws below stay inside these ranges and needn't reach their ends.
Inputs may be any that keep to these rules, and one draw needn't show every extreme that they name: `pattern`: 0 or 1; each device's block of 4 x 2 tiles holds 1 to 4 ones, and some block holds exactly 4.
All inputs are finite; a program needn't handle non-finite values.
Results may differ from the reference program's by a relative error of at most 0.0003.
Values may be sent and summed in bfloat16 or wider, within the bound.
A program may use at most 128 MiB of HBM per device.

```python
import math
import jax
import jax.numpy as jnp

TILE = 256
TC_DEV = 2
MOST = 4
TR_DEV = 4
N = 8192
TN = 32
P_SIZE = 8192


def draw_weights(key, part):
    key = jax.random.fold_in(key, 11)
    first, second, third = jax.random.split(key, 3)
    magnitude = jnp.exp(1.2 * jnp.clip(jax.random.normal(first, (N, N), jnp.float32), -4.0, 4.0))
    keep = jax.random.uniform(second, (N, N), jnp.float32) < 0.4
    row_scale = jnp.exp(jax.random.uniform(third, (N, 1), jnp.float32, 0.0, math.log(10.0)))
    return (jnp.where(keep, magnitude, 0.0) * row_scale).astype(jnp.bfloat16)


def draw_pattern(key, part):
    key = jax.random.fold_in(key, 23)
    first, second, third, fourth = jax.random.split(key, 4)
    block_rows = TN // TR_DEV
    block_cols = TN // TC_DEV
    counts = jax.random.randint(first, (block_rows, block_cols), 1, MOST + 1)
    pick_r = jax.random.randint(second, (), 0, block_rows)
    pick_c = jax.random.randint(third, (), 0, block_cols)
    counts = counts.at[pick_r, pick_c].set(MOST)
    per_block = TR_DEV * TC_DEV
    scores = jax.random.randint(fourth, (block_rows, block_cols, per_block), 0, 1 << 20)
    scores = scores * per_block + jnp.arange(per_block, dtype=jnp.int32)[None, None, :]
    ranks = jnp.argsort(jnp.argsort(scores, axis=-1), axis=-1)
    live = (ranks < counts[:, :, None]).astype(jnp.int32)
    live = live.reshape(block_rows, block_cols, TR_DEV, TC_DEV).transpose(0, 2, 1, 3)
    return live.reshape(TN, TN)


def levels(key, extent, cuts, least, largest):
    factor_of, own = 1.0, jax.random.fold_in(key, 6)
    for dim, blocks in cuts:
        heights = jnp.exp(jax.random.uniform(jax.random.fold_in(own, dim), (blocks,), jnp.float32, least / len(cuts), largest / len(cuts)))
        factor_of = factor_of * jnp.repeat(heights, extent[dim] // blocks).reshape([-1 if axis == dim else 1 for axis in range(len(extent))])
    return factor_of


def setup_inputs(seed: int = 0) -> dict:
    streams_of = jax.random.split(jax.random.key(seed), 4)
    weights = draw_weights(jax.random.fold_in(streams_of[3], 71), 0)
    panel = jnp.clip(jnp.exp(math.log(1.0) - 4.61031033 * jax.random.uniform(streams_of[1], (N, P_SIZE), jnp.float32) ** levels(streams_of[1], (N, P_SIZE), ((0, 8), (1, 16)), -0.2, 0.2)), 0.0099487305, 1.0).astype(jnp.bfloat16)
    pattern = draw_pattern(jax.random.fold_in(streams_of[3], 71), 0)
    return {"weights": weights, "panel": panel, "pattern": pattern}


def reference(weights, panel, pattern):
    grown = jnp.repeat(jnp.repeat(pattern, TILE, axis=0), TILE, axis=1)
    masked = weights * grown.astype(jnp.bfloat16)
    expanded = jnp.dot(masked, panel, preferred_element_type=jnp.float32)
    inflated = expanded * expanded
    totals = jnp.sum(inflated, axis=0)
    nodes = jnp.float32(weights.shape[0])
    return nodes * inflated / totals[None, :]
```

```python
import functools

import jax
import jax.numpy as jnp
from jax import lax
from jax.experimental import pallas as pl
from jax.experimental.pallas import tpu as pltpu
from jax.sharding import PartitionSpec as P

TILE = 256
MESH = pl.DeviceIdType.MESH
SIDE = 4
SLOTS = 4
COMPUTE = True

TREE = (
    ((1, 0), (0, 0)),
    ((-1, 0), (0, 0)),
    ((0, 1), (0, 0)),
    ((0, -1), (0, 0)),
    ((1, 1), (1, 0)),
    ((-1, -1), (-1, 0)),
    ((-1, 1), (0, 1)),
    ((1, -1), (0, -1)),
    ((2, 1), (1, 1)),
    ((-1, 2), (-1, 1)),
    ((2, -1), (1, -1)),
    ((1, 2), (1, 1)),
    ((2, 0), (1, 0)),
    ((0, 2), (0, 1)),
    ((2, 2), (2, 1)),
)
ROUNDS = len(TREE)
LAG = 3
STEPS = 6
UP = (0, 1, 2, 3, 0, 1)
DOWN = (2, 3, 0, 1, 2, 3)


def turn(offset, times):
    dx, dz = offset
    for _ in range(times):
        dx, dz = -dz, dx
    return dx, dz


def handled(step):
    return 2 * step + 1


def compute_plan():
    arrive = {(0, 0): 2}
    for number, (offset, _) in enumerate(TREE):
        for s in range(SLOTS):
            dx, dz = turn(offset, s)
            key = (dx % SIDE, dz % SIDE)
            arrive[key] = max(arrive.get(key, 0), number + 1 + LAG)
    last = ROUNDS + LAG
    orders = {}
    ready = {}
    for delta in range(SIDE):
        for parity in range(2):
            when = {}
            for (dx, dz), t in arrive.items():
                dy = (delta - dz) % SIDE
                quarter = (parity + dx) % 2
                if dy == 0:
                    b = 3
                elif dy == 2:
                    b = handled(6) + 1
                elif dy == 3:
                    b = handled(2 if quarter == 0 else 4) + 1
                else:
                    b = handled(2 if quarter == 1 else 4) + 1
                when[(dx, dz)] = max(t, b)
            order = sorted(when, key=lambda o: (when[o], o))
            orders[delta, parity] = order
            ready[delta, parity] = [when[o] for o in order]
    counts = {}
    done = 0
    for t in range(1, last + 1):
        able = min(sum(1 for w in ready[v] if w <= t) for v in ready) - done
        take = able if t > ROUNDS else min(able, 2)
        counts[t] = take
        done += take
    assert done == SIDE * SIDE
    return orders, counts


ORDERS, COUNTS = compute_plan()


def kernel(
    pattern_ref, weights_ref, panel_ref, out_ref, sums_ref,
    own, graph, panel, meta, total, part, parts,
    local_sem, out_sem, a_send, a_recv, b_send, b_recv, c_send, c_recv,
    m_send, m_recv, t_send, t_recv,
):
    row, col = lax.axis_index("row"), lax.axis_index("col")
    y, core = row // 2, row % 2
    z, x = col // SIDE, col % SIDE

    def wrap(v):
        return (v + 2 * SIDE) % SIDE

    def at(dx, dz):
        return wrap(z + dz) * SIDE + wrap(x + dx)

    def lane(dy):
        return wrap(y + dy) * 2 + core

    other = y * 2 + 1 - core

    load_a = pltpu.make_async_copy(weights_ref, own, local_sem.at[0])
    load_a.start()
    mine = pl.multiple_of(row * 4, 4)
    load_b = pltpu.make_async_copy(panel_ref, panel.at[pl.ds(mine, 4)], local_sem.at[1])
    load_b.start()

    barrier = pltpu.get_barrier_semaphore()
    for i in range(1, 16):
        pl.semaphore_signal(barrier, inc=1, device_id=(row, (col + i) % 16), device_id_type=MESH)
    for i in range(1, 8):
        pl.semaphore_signal(barrier, inc=1, device_id=((row + i) % 8, col), device_id_type=MESH)

    bits = [pattern_ref[i // 2, i % 2] for i in range(8)]
    code = functools.reduce(lambda a, b: a + b, [bits[i] << i for i in range(8)])
    meta[col, 0] = code

    load_a.wait()
    ranks = [jnp.int32(0)]
    for i in range(7):
        ranks.append(ranks[-1] + bits[i])
    for s in range(SLOTS):
        tile = jnp.zeros((TILE, TILE), jnp.bfloat16)
        for i in range(s, 8):
            r, c = i // 2 * TILE, i % 2 * TILE
            tile = jnp.where((bits[i] == 1) & (ranks[i] == s), own[r:r + TILE, c:c + TILE], tile)
        graph[col, s] = tile
    load_b.wait()
    pl.semaphore_wait(barrier, 22)

    def meta_copy(i):
        return pltpu.make_async_remote_copy(
            src_ref=meta.at[col], dst_ref=meta.at[col],
            send_sem=m_send.at[i - 1], recv_sem=m_recv.at[i - 1],
            device_id=(row, (col + i) % 16), device_id_type=MESH)

    def meta_arrival(i):
        source = (col - i + 16) % 16
        return pltpu.make_async_remote_copy(
            src_ref=meta.at[source], dst_ref=meta.at[source],
            send_sem=m_send.at[i - 1], recv_sem=m_recv.at[i - 1],
            device_id=(row, source), device_id_type=MESH)

    def a_copy(number, s):
        offset, parent = TREE[number]
        px, pz = turn(parent, s)
        dx, dz = turn((offset[0] - parent[0], offset[1] - parent[1]), s)
        source = at(-px, -pz)
        return pltpu.make_async_remote_copy(
            src_ref=graph.at[source, s], dst_ref=graph.at[source, s],
            send_sem=a_send.at[number, s], recv_sem=a_recv.at[number, s],
            device_id=(row, at(dx, dz)), device_id_type=MESH)

    def a_arrival(number, s):
        offset, _ = TREE[number]
        dx, dz = turn(offset, s)
        source = at(-dx, -dz)
        return pltpu.make_async_remote_copy(
            src_ref=graph.at[source, s], dst_ref=graph.at[source, s],
            send_sem=a_send.at[number, s], recv_sem=a_recv.at[number, s],
            device_id=(row, col), device_id_type=MESH)

    def b_piece(way, step, received):
        j = (UP if way > 0 else DOWN)[step - 1]
        hops = (1 if received else 0) + (1 if step > 4 else 0)
        return lane(-way * hops) * 4 + j

    def b_copy(way, step):
        piece = b_piece(way, step, False)
        n = 0 if way > 0 else 1
        return pltpu.make_async_remote_copy(
            src_ref=panel.at[piece], dst_ref=panel.at[piece],
            send_sem=b_send.at[step - 1, n], recv_sem=b_recv.at[step - 1, n],
            device_id=(lane(way), col), device_id_type=MESH)

    def b_arrival(way, step):
        piece = b_piece(way, step, True)
        n = 0 if way > 0 else 1
        return pltpu.make_async_remote_copy(
            src_ref=panel.at[piece], dst_ref=panel.at[piece],
            send_sem=b_send.at[step - 1, n], recv_sem=b_recv.at[step - 1, n],
            device_id=(row, col), device_id_type=MESH)

    def c_piece(step, n, theirs):
        if step == 0:
            lane_row, j = lane(0), n
        else:
            way = 1 if n == 0 else -1
            hops = 2 if step > 4 else 1
            lane_row, j = lane(-way * hops), (UP if way > 0 else DOWN)[step - 1]
        if theirs:
            lane_row = (lane_row // 2) * 2 + 1 - core
        return lane_row * 4 + j

    def c_copy(step, n, theirs=False):
        piece = c_piece(step, n, theirs)
        k = n if step == 0 else 2 + 2 * step + n
        return pltpu.make_async_remote_copy(
            src_ref=panel.at[piece], dst_ref=panel.at[piece],
            send_sem=c_send.at[k], recv_sem=c_recv.at[k],
            device_id=(other, col), device_id_type=MESH)

    def c_range(step):
        return range(4 if step == 0 else 2)

    def ordered(place):
        index = jnp.int32(0)
        variant = wrap(z - y) * 2 + x % 2
        for v in range(8):
            dx, dz = ORDERS[v // 2, v % 2][place]
            index = jnp.where(variant == v, at(-dx, -dz), index)
        return index

    def add_source(source, first):
        present = meta[source, 0]
        have = [(present >> i) & 1 for i in range(8)]
        before = [jnp.int32(0)]
        for i in range(7):
            before.append(before[-1] + have[i])
        tiles = [graph.at[source, s] for s in range(SLOTS)]
        piece = pl.multiple_of(source * 2, 2)
        for r in range(4):
            sides = []
            for c in range(2):
                i = 2 * r + c
                tile = jnp.zeros((TILE, TILE), jnp.bfloat16)
                for s in range(min(i + 1, SLOTS)):
                    tile = jnp.where((have[i] == 1) & (before[i] == s), tiles[s][...], tile)
                sides.append(tile)
            product = jnp.dot(sides[0], panel[piece], preferred_element_type=jnp.float32)
            product += jnp.dot(sides[1], panel[piece + 1], preferred_element_type=jnp.float32)
            rows = pl.ds(r * TILE, TILE)
            if first:
                total[rows, :] = product
            else:
                total[rows, :] += product

    done = 0
    for t in range(1, ROUNDS + LAG + 1):
        if t == 1:
            for i in range(1, 16):
                meta_copy(i).start()
        if t > LAG:
            for s in range(SLOTS):
                a_arrival(t - LAG - 1, s).wait_recv()
        if t <= ROUNDS:
            for s in range(SLOTS):
                a_copy(t - 1, s).start()
        if t == 1:
            for step in (1, 2):
                for way in (1, -1):
                    b_copy(way, step).start()
            for n in c_range(0):
                c_copy(0, n).start()
        if t == 2:
            for n in c_range(0):
                c_copy(0, n, True).wait_recv()
            for i in range(1, 16):
                meta_arrival(i).wait_recv()
        for step in range(1, STEPS + 1):
            if t == handled(step):
                for way in (1, -1):
                    b_arrival(way, step).wait_recv()
                for n in c_range(step):
                    c_copy(step, n).start()
                if step + 2 <= STEPS:
                    for way in (1, -1):
                        b_copy(way, step + 2).start()
            if t == handled(step) + 1:
                for n in c_range(step):
                    c_copy(step, n, True).wait_recv()
        for _ in range(COUNTS[t]):
            if COMPUTE:
                add_source(ordered(done), done == 0)
            done += 1

    def t_copy(i):
        return pltpu.make_async_remote_copy(
            src_ref=part, dst_ref=parts.at[row],
            send_sem=t_send.at[i - 1], recv_sem=t_recv.at[i - 1],
            device_id=((row + i) % 8, col), device_id_type=MESH)

    def t_arrival(i):
        source = (row - i + 8) % 8
        return pltpu.make_async_remote_copy(
            src_ref=part, dst_ref=parts.at[source],
            send_sem=t_send.at[i - 1], recv_sem=t_recv.at[i - 1],
            device_id=(row, col), device_id_type=MESH)

    sums = jnp.zeros((8, 512), jnp.float32)
    for r in range(4):
        block = total[r * TILE:(r + 1) * TILE, :]
        block = block * block
        total[r * TILE:(r + 1) * TILE, :] = block
        sums += jnp.sum(block.reshape(TILE // 8, 8, 512), axis=0)
    part[...] = sums
    for i in range(1, 8):
        t_copy(i).start()
    store = pltpu.make_async_copy(total, out_ref, out_sem)
    store.start()
    parts[row] = sums

    for i in range(1, 16):
        meta_copy(i).wait_send()
    for number in range(ROUNDS):
        for s in range(SLOTS):
            a_copy(number, s).wait_send()
    for step in range(1, STEPS + 1):
        for way in (1, -1):
            b_copy(way, step).wait_send()
    for step in range(STEPS + 1):
        for n in c_range(step):
            c_copy(step, n).wait_send()

    for i in range(1, 8):
        t_arrival(i).wait_recv()
    whole = parts[0]
    for i in range(1, 8):
        whole += parts[i]
    sums_ref[...] = jnp.sum(whole, axis=0, keepdims=True)
    for i in range(1, 8):
        t_copy(i).wait_send()
    store.wait()


def local(weights, panel, pattern):
    inflated, totals = pl.pallas_call(
        kernel,
        out_shape=(
            jax.ShapeDtypeStruct((1024, 512), jnp.float32),
            jax.ShapeDtypeStruct((1, 512), jnp.float32),
        ),
        in_specs=[
            pl.BlockSpec(memory_space=pltpu.SMEM),
            pl.BlockSpec(memory_space=pl.ANY),
            pl.BlockSpec(memory_space=pl.ANY),
        ],
        out_specs=(
            pl.BlockSpec(memory_space=pl.ANY),
            pl.BlockSpec(memory_space=pltpu.VMEM),
        ),
        scratch_shapes=[
            pltpu.VMEM((1024, 512), jnp.bfloat16),
            pltpu.VMEM((16, SLOTS, TILE, TILE), jnp.bfloat16),
            pltpu.VMEM((32, TILE, 512), jnp.bfloat16),
            pltpu.SMEM((16, 128), jnp.int32),
            pltpu.VMEM((1024, 512), jnp.float32),
            pltpu.VMEM((8, 512), jnp.float32),
            pltpu.VMEM((8, 8, 512), jnp.float32),
            pltpu.SemaphoreType.DMA((2,)),
            pltpu.SemaphoreType.DMA,
            pltpu.SemaphoreType.DMA((ROUNDS, SLOTS)),
            pltpu.SemaphoreType.DMA((ROUNDS, SLOTS)),
            pltpu.SemaphoreType.DMA((STEPS, 2)),
            pltpu.SemaphoreType.DMA((STEPS, 2)),
            pltpu.SemaphoreType.DMA((4 + 2 * STEPS,)),
            pltpu.SemaphoreType.DMA((4 + 2 * STEPS,)),
            pltpu.SemaphoreType.DMA((15,)),
            pltpu.SemaphoreType.DMA((15,)),
            pltpu.SemaphoreType.DMA((7,)),
            pltpu.SemaphoreType.DMA((7,)),
        ],
        compiler_params=pltpu.CompilerParams(
            collective_id=0, has_side_effects=True, vmem_limit_bytes=40 * 1024 * 1024
        ),
        cost_estimate=pl.CostEstimate(
            flops=2 * 1024 * 8192 * 512, bytes_accessed=4 * 1024 * 1024, transcendentals=0
        ),
    )(pattern, weights, panel.reshape(4, TILE, 512))
    nodes = jnp.float32(8192)
    return nodes * inflated / totals


def solution(mesh):
    spec = P("row", "col")
    return jax.shard_map(local, mesh=mesh, in_specs=(spec, spec, spec), out_specs=spec, check_vma=False)
```

```python
import functools

import jax
import jax.numpy as jnp
from jax import lax
from jax.experimental import pallas as pl
from jax.experimental.pallas import tpu as pltpu
from jax.sharding import PartitionSpec as P

TILE = 256
MESH = pl.DeviceIdType.MESH
SIDE = 4
SLOTS = 4
COMPUTE = True

TREE = (
    ((1, 0), (0, 0)),
    ((-1, 0), (0, 0)),
    ((0, 1), (0, 0)),
    ((0, -1), (0, 0)),
    ((1, 1), (1, 0)),
    ((-1, -1), (-1, 0)),
    ((-1, 1), (0, 1)),
    ((1, -1), (0, -1)),
    ((2, 1), (1, 1)),
    ((1, 2), (1, 1)),
    ((-1, 2), (-1, 1)),
    ((2, -1), (1, -1)),
    ((2, 0), (1, 0)),
    ((0, 2), (0, 1)),
    ((2, 2), (2, 1)),
)
ROUNDS = len(TREE)
LAG = 4
STEPS = 6
UP = (0, 1, 2, 3, 0, 1)
DOWN = (2, 3, 0, 1, 2, 3)


for number, (_, parent) in enumerate(TREE):
    assert parent == (0, 0) or [o for o, _ in TREE].index(parent) <= number - LAG


def turn(offset, times):
    dx, dz = offset
    for _ in range(times):
        dx, dz = -dz, dx
    return dx, dz


def handled(step):
    return 2 * step + 1


def compute_plan():
    arrive = {(0, 0): 2}
    for number, (offset, _) in enumerate(TREE):
        for s in range(SLOTS):
            dx, dz = turn(offset, s)
            key = (dx % SIDE, dz % SIDE)
            arrive[key] = max(arrive.get(key, 0), number + 1 + LAG)
    last = ROUNDS + LAG
    orders = {}
    ready = {}
    for delta in range(SIDE):
        for parity in range(2):
            when = {}
            for (dx, dz), t in arrive.items():
                dy = (delta - dz) % SIDE
                quarter = (parity + dx) % 2
                if dy == 0:
                    b = 3
                elif dy == 2:
                    b = handled(6) + 1
                elif dy == 3:
                    b = handled(2 if quarter == 0 else 4) + 1
                else:
                    b = handled(2 if quarter == 1 else 4) + 1
                when[(dx, dz)] = max(t, b)
            order = sorted(when, key=lambda o: (when[o], o))
            orders[delta, parity] = order
            ready[delta, parity] = [when[o] for o in order]
    counts = {}
    done = 0
    for t in range(LAG + 1, last + 1):
        able = min(sum(1 for w in ready[v] if w <= t) for v in ready) - done
        take = able if t > ROUNDS else min(able, 2)
        counts[t] = take
        done += take
    assert done == SIDE * SIDE
    return orders, counts


ORDERS, COUNTS = compute_plan()


def kernel(
    pattern_ref, weights_ref, panel_ref, total, sums_ref,
    own, graph, panel, pattern, meta, part, parts, local_sem,
    a_send, a_recv, b_send, b_recv, c_send, c_recv, m_send, m_recv, t_send, t_recv,
):
    row, col = lax.axis_index("row"), lax.axis_index("col")
    y, core = row // 2, row % 2
    z, x = col // SIDE, col % SIDE

    def wrap(v):
        return (v + 2 * SIDE) % SIDE

    def at(dx, dz):
        return wrap(z + dz) * SIDE + wrap(x + dx)

    def lane(dy):
        return wrap(y + dy) * 2 + core

    other = y * 2 + 1 - core

    load_a = pltpu.make_async_copy(weights_ref, own, local_sem.at[0])
    load_p = pltpu.make_async_copy(pattern_ref, pattern, local_sem.at[1])
    mine = pl.multiple_of(row * 4, 4)
    load_b = pltpu.make_async_copy(panel_ref, panel.at[pl.ds(mine, 4)], local_sem.at[2])
    load_p.start()
    load_a.start()

    barrier = pltpu.get_barrier_semaphore()
    for peer in (
        (row, at(1, 0)), (row, at(-1, 0)), (row, at(0, 1)), (row, at(0, -1)),
        (lane(1), col), (lane(-1), col), (other, col),
    ):
        pl.semaphore_signal(barrier, inc=1, device_id=peer, device_id_type=MESH)

    load_b.start()

    load_p.wait()
    load_a.wait()
    bits = [pattern[i % 2, i // 2] for i in range(8)]
    meta[col, 0] = functools.reduce(lambda a, b: a + b, [bits[i] << i for i in range(8)])
    ranks = [jnp.int32(0)]
    for i in range(7):
        ranks.append(ranks[-1] + bits[i])

    def pack(s):
        tile = jnp.zeros((TILE, TILE), jnp.bfloat16)
        for i in range(s, 8):
            r, c = i // 2 * TILE, i % 2 * TILE
            tile = jnp.where((bits[i] == 1) & (ranks[i] == s), own[r:r + TILE, c:c + TILE], tile)
        graph[col, s] = tile

    def remote(source, target, send_sem, recv_sem, device):
        return pltpu.make_async_remote_copy(
            src_ref=source, dst_ref=target, send_sem=send_sem, recv_sem=recv_sem,
            device_id=device, device_id_type=MESH)

    def arrived(block, recv_sem):
        remote(block, block, recv_sem, recv_sem, (row, col)).wait_recv()

    def sent(block, send_sem):
        remote(block, block, send_sem, send_sem, (row, col)).wait_send()

    def a_copy(number, s):
        offset, parent = TREE[number]
        px, pz = turn(parent, s)
        dx, dz = turn((offset[0] - parent[0], offset[1] - parent[1]), s)
        tile = graph.at[at(-px, -pz), s]
        return remote(tile, tile, a_send, a_recv.at[number], (row, at(dx, dz)))

    def m_copy(number):
        offset, (px, pz) = TREE[number]
        code = meta.at[at(-px, -pz)]
        return remote(code, code, m_send, m_recv.at[number], (row, at(offset[0] - px, offset[1] - pz)))

    def a_wait(number):
        arrived(graph.at[col], a_recv.at[number])
        arrived(meta.at[col], m_recv.at[number])

    def b_copy(way, step):
        j = (UP if way > 0 else DOWN)[step - 1]
        piece = panel.at[lane(-way if step > 4 else 0) * 4 + j]
        return remote(piece, piece, b_send, b_recv.at[step - 1], (lane(way), col))

    def b_wait(step):
        arrived(panel.at[pl.ds(0, 2)], b_recv.at[step - 1])

    def c_copy(step, n):
        if step == 0:
            piece = panel.at[row * 4 + n]
        else:
            way = 1 if n == 0 else -1
            j = (UP if way > 0 else DOWN)[step - 1]
            piece = panel.at[lane(-way * (2 if step > 4 else 1)) * 4 + j]
        return remote(piece, piece, c_send, c_recv.at[step], (other, col))

    def c_range(step):
        return range(4 if step == 0 else 2)

    def c_wait(step):
        arrived(panel.at[pl.ds(0, len(c_range(step)))], c_recv.at[step])

    def ordered(place):
        index = jnp.int32(0)
        variant = wrap(z - y) * 2 + x % 2
        for v in range(8):
            dx, dz = ORDERS[v // 2, v % 2][place]
            index = jnp.where(variant == v, at(-dx, -dz), index)
        return index

    def add_source(source, first, last=False):
        sums = jnp.zeros((1, 512), jnp.float32)
        present = meta[source, 0]
        have = [(present >> i) & 1 for i in range(8)]
        before = [jnp.int32(0)]
        for i in range(7):
            before.append(before[-1] + have[i])
        tiles = [graph.at[source, s] for s in range(SLOTS)]
        piece = pl.multiple_of(source * 2, 2)
        for r in range(4):
            sides = []
            for c in range(2):
                i = 2 * r + c
                tile = jnp.zeros((TILE, TILE), jnp.bfloat16)
                for s in range(min(i + 1, SLOTS)):
                    tile = jnp.where((have[i] == 1) & (before[i] == s), tiles[s][...], tile)
                sides.append(tile)
            product = jnp.dot(sides[0], panel[piece], preferred_element_type=jnp.float32)
            product += jnp.dot(sides[1], panel[piece + 1], preferred_element_type=jnp.float32)
            rows = pl.ds(r * TILE, TILE)
            if last:
                product += total[rows, :]
                product *= product
                sums += jnp.sum(product, axis=0, keepdims=True)
                total[rows, :] = product
            elif first:
                total[rows, :] = product
            else:
                total[rows, :] += product
        return sums

    for s in range(SLOTS):
        pack(s)
        if s == 0:
            pl.semaphore_wait(barrier, 7)
        for number in range(4):
            a_copy(number, s).start()
    for number in range(4):
        m_copy(number).start()
    load_b.wait()
    for step in (1, 2):
        for way in (1, -1):
            b_copy(way, step).start()
    for n in c_range(0):
        c_copy(0, n).start()

    done = 0
    for t in range(LAG + 1, ROUNDS + LAG + 1):
        a_wait(t - LAG - 1)
        if t <= ROUNDS:
            for s in range(SLOTS):
                a_copy(t - 1, s).start()
            m_copy(t - 1).start()
        if t == LAG + 1:
            c_wait(0)
        for step in range(1, STEPS + 1):
            if t == max(handled(step), LAG + 1):
                b_wait(step)
                for n in c_range(step):
                    c_copy(step, n).start()
                if step + 2 <= STEPS:
                    for way in (1, -1):
                        b_copy(way, step + 2).start()
            if t == max(handled(step), LAG + 1) + 1:
                c_wait(step)
        for _ in range(COUNTS[t]):
            if COMPUTE and done < SIDE * SIDE - 1:
                add_source(ordered(done), done == 0)
            done += 1

    sums = add_source(ordered(done - 1), False, True)
    part[...] = sums
    for i in range(1, 8):
        remote(part, parts.at[row], t_send, t_recv, ((row + i) % 8, col)).start()
    parts[row] = sums

    sent(graph.at[pl.ds(0, ROUNDS)], a_send)
    sent(meta.at[pl.ds(0, ROUNDS)], m_send)
    sent(panel.at[pl.ds(0, 2 * STEPS)], b_send)
    sent(panel.at[pl.ds(0, 4 + 2 * STEPS)], c_send)

    arrived(parts.at[pl.ds(0, 7)], t_recv)
    whole = parts[0]
    for i in range(1, 8):
        whole += parts[i]
    sums_ref[...] = whole
    sent(parts.at[pl.ds(0, 7)], t_send)


def local(weights, panel, pattern):
    def stay(array):
        return pltpu.with_memory_space_constraint(array, pltpu.HBM)

    inflated, totals = pl.pallas_call(
        kernel,
        out_shape=(
            pltpu.VMEM((1024, 512), jnp.float32),
            pltpu.VMEM((1, 512), jnp.float32),
        ),
        in_specs=[pl.BlockSpec(memory_space=pltpu.HBM)] * 3,
        out_specs=(
            pl.BlockSpec(memory_space=pltpu.VMEM),
            pl.BlockSpec(memory_space=pltpu.VMEM),
        ),
        scratch_shapes=[
            pltpu.VMEM((1024, 512), jnp.bfloat16),
            pltpu.VMEM((16, SLOTS, TILE, TILE), jnp.bfloat16),
            pltpu.VMEM((32, TILE, 512), jnp.bfloat16),
            pltpu.SMEM((2, 4), jnp.int32),
            pltpu.SMEM((16, 128), jnp.int32),
            pltpu.VMEM((1, 512), jnp.float32),
            pltpu.VMEM((8, 1, 512), jnp.float32),
            pltpu.SemaphoreType.DMA((3,)),
            pltpu.SemaphoreType.DMA,
            pltpu.SemaphoreType.DMA((ROUNDS,)),
            pltpu.SemaphoreType.DMA,
            pltpu.SemaphoreType.DMA((STEPS,)),
            pltpu.SemaphoreType.DMA,
            pltpu.SemaphoreType.DMA((STEPS + 1,)),
            pltpu.SemaphoreType.DMA,
            pltpu.SemaphoreType.DMA((ROUNDS,)),
            pltpu.SemaphoreType.DMA,
            pltpu.SemaphoreType.DMA,
        ],
        compiler_params=pltpu.CompilerParams(
            collective_id=0, has_side_effects=True, vmem_limit_bytes=40 * 1024 * 1024
        ),
        cost_estimate=pl.CostEstimate(
            flops=2 * 1024 * 8192 * 512, bytes_accessed=4 * 1024 * 1024, transcendentals=0
        ),
    )(stay(pattern.T), stay(weights), stay(panel.reshape(4, TILE, 512)))
    nodes = jnp.float32(8192)
    return nodes * inflated / totals


def solution(mesh):
    spec = P("row", "col")
    return jax.shard_map(local, mesh=mesh, in_specs=(spec, spec, spec), out_specs=spec, check_vma=False)
```

```python
import functools

import jax
import jax.numpy as jnp
from jax import lax
from jax.experimental import pallas as pl
from jax.experimental.pallas import tpu as pltpu
from jax.sharding import PartitionSpec as P

TILE = 256
MESH = pl.DeviceIdType.MESH
SIDE = 4
SLOTS = 4
STEPS = 3
UP = (0, 2, 0)
DOWN = (2, 0, 2)


def turn(offset, times):
    dx, dz = offset
    for _ in range(times):
        dx, dz = -dz, dx
    return dx, dz


def around(offset, parent, first):
    return [(turn(offset, k), turn(parent, k), first, 2) for k in range(4)]


PHASES = (
    around((1, 0), (0, 0), 0),
    around((1, 0), (0, 0), 2),
    around((1, 1), (1, 0), 0),
    around((1, 1), (1, 0), 2),
    around((2, 1), (1, 1), 0),
    around((2, 1), (1, 1), 2),
    [((2, 0), (1, 0), 0, 2), ((2, 0), (-1, 0), 2, 2), ((0, 2), (0, 1), 0, 2), ((0, 2), (0, -1), 2, 2)],
    [((2, 2), (2, 1), 0, 1), ((2, 2), (2, -1), 1, 1), ((2, 2), (1, 2), 2, 1), ((2, 2), (-1, 2), 3, 1)],
)
CODES = {
    1: [leg[:2] for leg in PHASES[1]],
    3: [leg[:2] for leg in PHASES[3]],
    5: [leg[:2] for leg in PHASES[5]],
    6: [((2, 0), (1, 0)), ((0, 2), (0, 1))],
    7: [((2, 2), (2, 1))],
}
MOMENTS = (
    ("a", 0), ("c", 0), ("a", 1), ("b", 1), ("a", 2), ("c", 1), ("a", 3), ("b", 2),
    ("a", 4), ("c", 2), ("a", 5), ("b", 3), ("c", 3), ("a", 6), ("a", 7),
)


def compute_plan():
    when = {moment: i for i, moment in enumerate(MOMENTS)}
    arrive = {(0, 0): 0}
    for number, legs in enumerate(PHASES):
        for (dx, dz), _, _, _ in legs:
            arrive[dx % SIDE, dz % SIDE] = when["a", number]
    orders, ready = {}, {}
    for delta in range(SIDE):
        for parity in range(2):
            able = {}
            for (dx, dz), moment in arrive.items():
                dy = (delta - dz) % SIDE
                quarter = (parity + dx) % 2
                step = {0: 0, 2: 3, 3: 1 + quarter, 1: 2 - quarter}[dy]
                able[dx, dz] = max(moment, when["c", step])
            order = sorted(able, key=lambda o: (able[o], o))
            orders[delta, parity] = order
            ready[delta, parity] = [able[o] for o in order]
    counts, done = [], 0
    for i in range(len(MOMENTS)):
        take = min(sum(1 for w in ready[v] if w <= i) for v in ready) - done
        counts.append(take)
        done += take
    assert done == SIDE * SIDE and counts[-1] == 1
    return orders, counts


ORDERS, COUNTS = compute_plan()


def kernel(
    pattern_ref, weights_ref, panel_ref, total, sums_ref,
    own, graph, panel, pattern, meta, part, parts, local_sem,
    a_send, a_recv, b_send, b_recv, c_send, c_recv, m_send, m_recv, t_send, t_recv,
):
    row, col = lax.axis_index("row"), lax.axis_index("col")
    y, core = row // 2, row % 2
    z, x = col // SIDE, col % SIDE

    def wrap(v):
        return (v + 2 * SIDE) % SIDE

    def at(dx, dz):
        return wrap(z + dz) * SIDE + wrap(x + dx)

    def lane(dy):
        return wrap(y + dy) * 2 + core

    other = y * 2 + 1 - core

    load_p = pltpu.make_async_copy(pattern_ref, pattern, local_sem.at[1])
    mine = pl.multiple_of(row * 4, 4)
    load_b = pltpu.make_async_copy(panel_ref, panel.at[pl.ds(mine, 4)], local_sem.at[2])
    load_p.start()
    for i in range(4):
        rows = pl.ds(i * TILE, TILE)
        pltpu.make_async_copy(weights_ref.at[rows], own.at[rows], local_sem.at[0]).start()

    barrier = pltpu.get_barrier_semaphore()
    for peer in (
        (row, at(1, 0)), (row, at(-1, 0)), (row, at(0, 1)), (row, at(0, -1)),
        (lane(1), col), (lane(-1), col), (other, col),
    ):
        pl.semaphore_signal(barrier, inc=1, device_id=peer, device_id_type=MESH)


    load_p.wait()
    pltpu.make_async_copy(weights_ref, own, local_sem.at[0]).wait()
    load_b.start()
    bits = [pattern[i % 2, i // 2] for i in range(8)]
    meta[col, 0] = functools.reduce(lambda a, b: a + b, [bits[i] << i for i in range(8)])
    ranks = [jnp.int32(0)]
    for i in range(7):
        ranks.append(ranks[-1] + bits[i])

    def pack(s):
        tile = jnp.zeros((TILE, TILE), jnp.bfloat16)
        for i in range(s, 8):
            r, c = i // 2 * TILE, i % 2 * TILE
            tile = jnp.where((bits[i] == 1) & (ranks[i] == s), own[r:r + TILE, c:c + TILE], tile)
        graph[col, s] = tile

    def remote(source, target, send_sem, recv_sem, device):
        return pltpu.make_async_remote_copy(
            src_ref=source, dst_ref=target, send_sem=send_sem, recv_sem=recv_sem,
            device_id=device, device_id_type=MESH)

    def arrived(block, recv_sem):
        remote(block, block, recv_sem, recv_sem, (row, col)).wait_recv()

    def sent(block, send_sem):
        remote(block, block, send_sem, send_sem, (row, col)).wait_send()

    def send(number):
        for (dx, dz), (px, pz), first, count in PHASES[number]:
            tiles = graph.at[at(-px, -pz), pl.ds(first, count)]
            remote(tiles, tiles, a_send, a_recv.at[number], (row, at(dx - px, dz - pz))).start()

    def send_codes(number):
        for (dx, dz), (px, pz) in CODES[number]:
            code = meta.at[at(-px, -pz)]
            remote(code, code, m_send, m_recv.at[number], (row, at(dx - px, dz - pz))).start()

    def a_wait(number):
        count = sum(leg[3] for leg in PHASES[number]) // SLOTS
        arrived(graph.at[pl.ds(0, count)], a_recv.at[number])
        if number in CODES:
            arrived(meta.at[pl.ds(0, len(CODES[number]))], m_recv.at[number])

    def two(device_row, j):
        return panel.at[pl.ds(device_row * 4 + j, 2)]

    def b_copy(way, step):
        pieces = two(lane(-way if step == STEPS else 0), (UP if way > 0 else DOWN)[step - 1])
        return remote(pieces, pieces, b_send, b_recv.at[step - 1], (lane(way), col))

    def b_wait(step):
        arrived(panel.at[pl.ds(0, 4)], b_recv.at[step - 1])

    def c_copy(step, way):
        if step == 0:
            pieces = panel.at[pl.ds(mine, 4)]
        else:
            hops = 2 if step == STEPS else 1
            pieces = two(lane(-way * hops), (UP if way > 0 else DOWN)[step - 1])
        return remote(pieces, pieces, c_send, c_recv.at[step], (other, col))

    def c_wait(step):
        arrived(panel.at[pl.ds(0, 4)], c_recv.at[step])

    def ordered(place):
        index = jnp.int32(0)
        variant = wrap(z - y) * 2 + x % 2
        for v in range(8):
            dx, dz = ORDERS[v // 2, v % 2][place]
            index = jnp.where(variant == v, at(-dx, -dz), index)
        return index

    def add_source(source, first, last=False):
        sums = jnp.zeros((1, 512), jnp.float32)
        present = meta[source, 0]
        have = [(present >> i) & 1 for i in range(8)]
        before = [jnp.int32(0)]
        for i in range(7):
            before.append(before[-1] + have[i])
        tiles = [graph.at[source, s] for s in range(SLOTS)]
        piece = pl.multiple_of(source * 2, 2)
        for r in range(4):
            sides = []
            for c in range(2):
                i = 2 * r + c
                tile = jnp.zeros((TILE, TILE), jnp.bfloat16)
                for s in range(min(i + 1, SLOTS)):
                    tile = jnp.where((have[i] == 1) & (before[i] == s), tiles[s][...], tile)
                sides.append(tile)
            product = jnp.dot(sides[0], panel[piece], preferred_element_type=jnp.float32)
            product += jnp.dot(sides[1], panel[piece + 1], preferred_element_type=jnp.float32)
            rows = pl.ds(r * TILE, TILE)
            if last:
                product += total[rows, :]
                product *= product
                sums += jnp.sum(product, axis=0, keepdims=True)
                total[rows, :] = product
            elif first:
                total[rows, :] = product
            else:
                total[rows, :] += product
        return sums

    pack(0)
    pack(1)
    pl.semaphore_wait(barrier, 7)
    send(0)
    pack(2)
    pack(3)
    send(1)
    send_codes(1)
    load_b.wait()
    for step in (1, 2):
        for way in (1, -1):
            b_copy(way, step).start()
    c_copy(0, 1).start()

    done = 0
    for (kind, number), count in zip(MOMENTS, COUNTS):
        if kind == "a":
            a_wait(number)
            for later in {0: (2,), 1: (3,), 2: (4,), 3: (5, 6), 5: (7,)}.get(number, ()):
                send(later)
                if later in CODES:
                    send_codes(later)
        elif kind == "b":
            b_wait(number)
            for way in (1, -1):
                c_copy(number, way).start()
            if number + 2 <= STEPS:
                for way in (1, -1):
                    b_copy(way, number + 2).start()
        else:
            c_wait(number)
        for _ in range(count):
            if done < SIDE * SIDE - 1:
                add_source(ordered(done), done == 0)
            done += 1

    sums = add_source(ordered(done - 1), False, True)
    part[...] = sums
    for i in range(1, 8):
        remote(part, parts.at[row], t_send, t_recv, ((row + i) % 8, col)).start()
    parts[row] = sums

    sent(graph.at[pl.ds(0, 15)], a_send)
    sent(meta.at[pl.ds(0, 15)], m_send)
    sent(panel.at[pl.ds(0, 4 * STEPS)], b_send)
    sent(panel.at[pl.ds(0, 4 + 4 * STEPS)], c_send)

    arrived(parts.at[pl.ds(0, 7)], t_recv)
    whole = parts[0]
    for i in range(1, 8):
        whole += parts[i]
    sums_ref[...] = whole
    sent(parts.at[pl.ds(0, 7)], t_send)


def divide(inflated_ref, totals_ref, flow_ref, held, sem):
    size = 1024 // 8
    for i in range(8):
        rows = pl.ds(i * size, size)
        held[rows, :] = jnp.float32(8192) * inflated_ref[rows, :] / totals_ref[...]
        pltpu.make_async_copy(held.at[rows], flow_ref.at[rows], sem).start()
    pltpu.make_async_copy(held, flow_ref, sem).wait()


def local(weights, panel, pattern):
    def stay(array):
        return pltpu.with_memory_space_constraint(array, pltpu.HBM)

    inflated, totals = pl.pallas_call(
        kernel,
        out_shape=(
            pltpu.VMEM((1024, 512), jnp.float32),
            pltpu.VMEM((1, 512), jnp.float32),
        ),
        in_specs=[pl.BlockSpec(memory_space=pltpu.HBM)] * 3,
        out_specs=(
            pl.BlockSpec(memory_space=pltpu.VMEM),
            pl.BlockSpec(memory_space=pltpu.VMEM),
        ),
        scratch_shapes=[
            pltpu.VMEM((1024, 512), jnp.bfloat16),
            pltpu.VMEM((16, SLOTS, TILE, TILE), jnp.bfloat16),
            pltpu.VMEM((32, TILE, 512), jnp.bfloat16),
            pltpu.SMEM((2, 4), jnp.int32),
            pltpu.SMEM((16, 128), jnp.int32),
            pltpu.VMEM((1, 512), jnp.float32),
            pltpu.VMEM((8, 1, 512), jnp.float32),
            pltpu.SemaphoreType.DMA((3,)),
            pltpu.SemaphoreType.DMA,
            pltpu.SemaphoreType.DMA((len(PHASES),)),
            pltpu.SemaphoreType.DMA,
            pltpu.SemaphoreType.DMA((STEPS,)),
            pltpu.SemaphoreType.DMA,
            pltpu.SemaphoreType.DMA((STEPS + 1,)),
            pltpu.SemaphoreType.DMA,
            pltpu.SemaphoreType.DMA((len(PHASES),)),
            pltpu.SemaphoreType.DMA,
            pltpu.SemaphoreType.DMA,
        ],
        compiler_params=pltpu.CompilerParams(
            collective_id=0, has_side_effects=True, vmem_limit_bytes=40 * 1024 * 1024
        ),
        cost_estimate=pl.CostEstimate(
            flops=2 * 1024 * 8192 * 512, bytes_accessed=4 * 1024 * 1024, transcendentals=0
        ),
    )(stay(pattern.T), stay(weights), stay(panel.reshape(4, TILE, 512)))
    return pl.pallas_call(
        divide,
        out_shape=jax.ShapeDtypeStruct((1024, 512), jnp.float32),
        in_specs=[pl.BlockSpec(memory_space=pltpu.VMEM)] * 2,
        out_specs=pl.BlockSpec(memory_space=pltpu.HBM),
        scratch_shapes=[pltpu.VMEM((1024, 512), jnp.float32), pltpu.SemaphoreType.DMA],
        compiler_params=pltpu.CompilerParams(vmem_limit_bytes=16 * 1024 * 1024),
    )(
        pltpu.with_memory_space_constraint(inflated, pltpu.VMEM),
        pltpu.with_memory_space_constraint(totals, pltpu.VMEM),
    )


def solution(mesh):
    spec = P("row", "col")
    return jax.shard_map(local, mesh=mesh, in_specs=(spec, spec, spec), out_specs=spec, check_vma=False)
```

```python
import functools

import jax
import jax.numpy as jnp
from jax import lax
from jax.experimental import pallas as pl
from jax.experimental.pallas import tpu as pltpu
from jax.sharding import PartitionSpec as P

TILE = 256
HALF = 128
MESH = pl.DeviceIdType.MESH
SIDE = 4
SLOTS = 4
STEPS = 3
UP = (0, 2, 0)
DOWN = (2, 0, 2)


def turn(offset, times):
    dx, dz = offset
    for _ in range(times):
        dx, dz = -dz, dx
    return dx, dz


def around(offset, parent, first):
    return [(turn(offset, k), turn(parent, k), first, 2) for k in range(4)]


PHASES = (
    around((1, 0), (0, 0), 0),
    around((1, 0), (0, 0), 2),
    around((1, 1), (1, 0), 0),
    around((1, 1), (1, 0), 2),
    around((2, 1), (1, 1), 0),
    around((2, 1), (1, 1), 2),
    [((2, 0), (1, 0), 0, 2), ((2, 0), (-1, 0), 2, 2), ((0, 2), (0, 1), 0, 2), ((0, 2), (0, -1), 2, 2)],
    [((2, 2), (2, 1), 0, 1), ((2, 2), (2, -1), 1, 1), ((2, 2), (1, 2), 2, 1), ((2, 2), (-1, 2), 3, 1)],
    [((2, 2), (2, 1), 0, 1), ((2, 2), (2, -1), 1, 1), ((2, 2), (1, 2), 2, 1), ((2, 2), (-1, 2), 3, 1)],
)
CODES = {
    1: [leg[:2] for leg in PHASES[1]],
    3: [leg[:2] for leg in PHASES[3]],
    5: [leg[:2] for leg in PHASES[5]],
    6: [((2, 0), (1, 0)), ((0, 2), (0, 1))],
    7: [((2, 2), (2, 1))],
}
MOMENTS = (
    ("a", 0), ("c", 0), ("a", 1), ("b", 1), ("a", 2), ("c", 1), ("a", 3), ("b", 2),
    ("a", 4), ("c", 2), ("a", 5), ("b", 3), ("c", 3), ("a", 6), ("a", 7), ("a", 8),
)


def compute_plan():
    when = {moment: i for i, moment in enumerate(MOMENTS)}
    arrive = {(0, 0): 0}
    for number, legs in enumerate(PHASES):
        for (dx, dz), _, _, _ in legs:
            arrive[dx % SIDE, dz % SIDE] = when["a", number]
    orders, ready = {}, {}
    for delta in range(SIDE):
        for parity in range(2):
            able = {}
            for (dx, dz), moment in arrive.items():
                dy = (delta - dz) % SIDE
                quarter = (parity + dx) % 2
                step = {0: 0, 2: 3, 3: 1 + quarter, 1: 2 - quarter}[dy]
                able[dx, dz] = max(moment, when["c", step])
            order = sorted(able, key=lambda o: (able[o], o))
            orders[delta, parity] = order
            ready[delta, parity] = [able[o] for o in order]
    counts, done = [], 0
    for i in range(len(MOMENTS)):
        take = min(sum(1 for w in ready[v] if w <= i) for v in ready) - done
        counts.append(take)
        done += take
    assert done == SIDE * SIDE and counts[-1] == 1
    return orders, counts


ORDERS, COUNTS = compute_plan()


def kernel(
    pattern_ref, weights_ref, panel_ref, total, sums_ref,
    own, graph, panel, pattern, meta, part, parts, local_sem,
    a_send, a_recv, b_send, b_recv, c_send, c_recv, m_send, m_recv, t_send, t_recv, both,
):
    row, col = lax.axis_index("row"), lax.axis_index("col")
    y, core = row // 2, row % 2
    z, x = col // SIDE, col % SIDE

    def wrap(v):
        return (v + 2 * SIDE) % SIDE

    def at(dx, dz):
        return wrap(z + dz) * SIDE + wrap(x + dx)

    def lane(dy):
        return wrap(y + dy) * 2 + core

    def lane_of(dy, which):
        return wrap(y + dy) * 2 + which

    other = y * 2 + 1 - core

    load_p = pltpu.make_async_copy(pattern_ref, pattern, local_sem.at[1])
    mine = pl.multiple_of(row * 4, 4)
    load_b = pltpu.make_async_copy(panel_ref, panel.at[pl.ds(mine, 4)], local_sem.at[2])
    load_p.start()
    for i in range(4):
        rows = pl.ds(i * TILE, TILE)
        pltpu.make_async_copy(weights_ref.at[rows], own.at[rows], local_sem.at[0]).start()

    barrier = pltpu.get_barrier_semaphore()
    for sign in (1, -1):
        for peer in (
            (lane_of(0, 0), at(sign, 0)), (lane_of(0, 1), at(0, sign)), (lane(sign), col),
        ):
            pl.semaphore_signal(barrier, inc=1, device_id=peer, device_id_type=MESH)
    pl.semaphore_signal(barrier, inc=1, device_id=(other, col), device_id_type=MESH)

    load_p.wait()
    pltpu.make_async_copy(weights_ref, own, local_sem.at[0]).wait()
    load_b.start()
    bits = [pattern[i % 2, i // 2] for i in range(8)]
    meta[col, 0] = functools.reduce(lambda a, b: a + b, [bits[i] << i for i in range(8)])
    def places(have):
        gaps, extras = [jnp.int32(0)], [jnp.int32(0)]
        for i in range(3):
            gaps.append(gaps[-1] + 1 - have[i])
            extras.append(extras[-1] + have[4 + i])
        return [[(have[s] == 0) & (have[4 + i] == 1) & (gaps[s] == extras[i]) for i in range(4)] for s in range(SLOTS)]

    holds = places(bits)

    def pack(s):
        def tile(i):
            r, c = i // 2 * TILE, i % 2 * TILE
            return own[r:r + TILE, c:c + TILE]

        packed = tile(s)
        for i in range(4):
            packed = jnp.where(holds[s][i], tile(4 + i), packed)
        graph[col, s] = packed

    def remote(source, target, send_sem, recv_sem, device):
        return pltpu.make_async_remote_copy(
            src_ref=source, dst_ref=target, send_sem=send_sem, recv_sem=recv_sem,
            device_id=device, device_id_type=MESH)

    def arrived(block, recv_sem):
        remote(block, block, recv_sem, recv_sem, (row, col)).wait_recv()

    def sent(block, send_sem):
        remote(block, block, send_sem, send_sem, (row, col)).wait_send()

    def send(number):
        for (dx, dz), (px, pz), first, count in PHASES[number]:
            tiles = graph.at[at(-px, -pz), pl.ds(first, count)]
            if number >= 7:
                tiles = tiles.at[:, pl.ds((number - 7) * HALF, HALF)]
            remote(tiles, tiles, a_send, a_recv.at[number], (row, at(dx - px, dz - pz))).start()

    def send_codes(number):
        for (dx, dz), (px, pz) in CODES[number]:
            code = meta.at[at(-px, -pz)]
            remote(code, code, m_send, m_recv.at[number], (row, at(dx - px, dz - pz))).start()

    def a_wait(number):
        if number >= 7:
            arrived(graph.at[0, pl.ds(0, 2)], a_recv.at[number])
        else:
            arrived(graph.at[pl.ds(0, 2)], a_recv.at[number])
        if number in CODES:
            arrived(meta.at[pl.ds(0, len(CODES[number]))], m_recv.at[number])

    def two(device_row, j):
        return panel.at[pl.ds(device_row * 4 + j, 2)]

    def b_copy(way, step):
        pieces = two(lane(-way if step == STEPS else 0), (UP if way > 0 else DOWN)[step - 1])
        return remote(pieces, pieces, b_send, b_recv.at[step - 1], (lane(way), col))

    def b_wait(step):
        arrived(panel.at[pl.ds(0, 4)], b_recv.at[step - 1])

    def c_copy(step, way):
        if step == 0:
            pieces = panel.at[pl.ds(mine, 4)]
        else:
            hops = 2 if step == STEPS else 1
            pieces = two(lane(-way * hops), (UP if way > 0 else DOWN)[step - 1])
        return remote(pieces, pieces, c_send, c_recv.at[step], (other, col))

    def c_wait(step):
        arrived(panel.at[pl.ds(0, 4)], c_recv.at[step])

    def ordered(place):
        index = jnp.int32(0)
        variant = wrap(z - y) * 2 + x % 2
        for v in range(8):
            dx, dz = ORDERS[v // 2, v % 2][place]
            index = jnp.where(variant == v, at(-dx, -dz), index)
        return index

    def product(source, have, holding, r, start, size):
        piece = pl.multiple_of(source * 2, 2)
        value = jnp.zeros((size, 512), jnp.float32)
        for c in range(2):
            i = 2 * r + c
            tile = jnp.zeros((size, TILE), jnp.bfloat16)
            for s in range(SLOTS) if i >= 4 else (i,):
                taken = holding[s][i - 4] if i >= 4 else have[i] == 1
                tile = jnp.where(taken, graph[source, s, start:start + size, :], tile)
            value += jnp.dot(tile, panel[piece + c], preferred_element_type=jnp.float32)
        return value

    def code(source):
        present = meta[source, 0]
        have = [(present >> i) & 1 for i in range(8)]
        return have, places(have)

    def add_source(source, first):
        have, holding = code(source)
        for r in range(4):
            rows = pl.ds(r * TILE, TILE)
            value = product(source, have, holding, r, 0, TILE)
            if first:
                total[rows, :] = value
            else:
                total[rows, :] += value

    def finish(source, half):
        have, holding = code(source)
        sums = jnp.zeros((1, 512), jnp.float32)
        for r in range(4):
            rows = pl.ds(r * TILE + half * HALF, HALF)
            value = total[rows, :] + product(source, have, holding, r, half * HALF, HALF)
            value = value * value
            total[rows, :] = value
            sums += jnp.sum(value, axis=0, keepdims=True)
        return sums

    def own_pair(number, along):
        for sign in (1, -1):
            tiles = graph.at[col, pl.ds(2 * number, 2)]
            target = at(sign * (1 - along), sign * along)
            remote(tiles, tiles, a_send, a_recv.at[number], (row, target)).start()

    pack(0)
    pack(1)
    pl.semaphore_wait(barrier, 7)
    pl.semaphore_signal(both, inc=1, device_id=(other, col), device_id_type=MESH)
    own_pair(0, core)
    pack(2)
    pack(3)
    pl.semaphore_wait(both, 1)
    own_pair(0, 1 - core)
    own_pair(1, core)
    own_pair(1, 1 - core)
    send_codes(1)
    load_b.wait()
    for step in (1, 2):
        for way in (1, -1):
            b_copy(way, step).start()
    c_copy(0, 1).start()

    done = 0
    sums = []
    for (kind, number), count in zip(MOMENTS, COUNTS):
        if kind == "a":
            a_wait(number)
            for later in {0: (2,), 1: (3,), 2: (4,), 3: (5, 6), 5: (7, 8)}.get(number, ()):
                send(later)
                if later in CODES:
                    send_codes(later)
        elif kind == "b":
            b_wait(number)
            for way in (1, -1):
                c_copy(number, way).start()
            if number + 2 <= STEPS:
                for way in (1, -1):
                    b_copy(way, number + 2).start()
        else:
            c_wait(number)
        for _ in range(count):
            if done < SIDE * SIDE - 1:
                add_source(ordered(done), done == 0)
            done += 1
        if kind == "a" and number >= 7:
            sums.append(finish(ordered(SIDE * SIDE - 1), number - 7))

    part[...] = sums[0] + sums[1]
    for i in range(1, 8):
        remote(part, parts.at[row], t_send, t_recv, ((row + i) % 8, col)).start()
    parts[row] = sums[0] + sums[1]

    sent(graph.at[pl.ds(0, 15)], a_send)
    sent(meta.at[pl.ds(0, 15)], m_send)
    sent(panel.at[pl.ds(0, 4 * STEPS)], b_send)
    sent(panel.at[pl.ds(0, 4 + 4 * STEPS)], c_send)

    arrived(parts.at[pl.ds(0, 7)], t_recv)
    whole = parts[0]
    for i in range(1, 8):
        whole += parts[i]
    sums_ref[...] = whole
    sent(parts.at[pl.ds(0, 7)], t_send)


def divide(inflated_ref, totals_ref, flow_ref, held, sem):
    size = 1024 // 8
    for i in range(8):
        rows = pl.ds(i * size, size)
        held[rows, :] = jnp.float32(8192) * inflated_ref[rows, :] / totals_ref[...]
        pltpu.make_async_copy(held.at[rows], flow_ref.at[rows], sem).start()
    pltpu.make_async_copy(held, flow_ref, sem).wait()


def local(weights, panel, pattern):
    def stay(array):
        return pltpu.with_memory_space_constraint(array, pltpu.HBM)

    inflated, totals = pl.pallas_call(
        kernel,
        out_shape=(
            pltpu.VMEM((1024, 512), jnp.float32),
            pltpu.VMEM((1, 512), jnp.float32),
        ),
        in_specs=[pl.BlockSpec(memory_space=pltpu.HBM)] * 3,
        out_specs=(
            pl.BlockSpec(memory_space=pltpu.VMEM),
            pl.BlockSpec(memory_space=pltpu.VMEM),
        ),
        scratch_shapes=[
            pltpu.VMEM((1024, 512), jnp.bfloat16),
            pltpu.VMEM((16, SLOTS, TILE, TILE), jnp.bfloat16),
            pltpu.VMEM((32, TILE, 512), jnp.bfloat16),
            pltpu.SMEM((2, 4), jnp.int32),
            pltpu.SMEM((16, 128), jnp.int32),
            pltpu.VMEM((1, 512), jnp.float32),
            pltpu.VMEM((8, 1, 512), jnp.float32),
            pltpu.SemaphoreType.DMA((3,)),
            pltpu.SemaphoreType.DMA,
            pltpu.SemaphoreType.DMA((len(PHASES),)),
            pltpu.SemaphoreType.DMA,
            pltpu.SemaphoreType.DMA((STEPS,)),
            pltpu.SemaphoreType.DMA,
            pltpu.SemaphoreType.DMA((STEPS + 1,)),
            pltpu.SemaphoreType.DMA,
            pltpu.SemaphoreType.DMA((len(PHASES),)),
            pltpu.SemaphoreType.DMA,
            pltpu.SemaphoreType.DMA,
            pltpu.SemaphoreType.REGULAR,
        ],
        compiler_params=pltpu.CompilerParams(
            collective_id=0, has_side_effects=True, vmem_limit_bytes=40 * 1024 * 1024
        ),
        cost_estimate=pl.CostEstimate(
            flops=2 * 1024 * 8192 * 512, bytes_accessed=4 * 1024 * 1024, transcendentals=0
        ),
    )(stay(pattern.T), stay(weights), stay(panel.reshape(4, TILE, 512)))
    return pl.pallas_call(
        divide,
        out_shape=jax.ShapeDtypeStruct((1024, 512), jnp.float32),
        in_specs=[pl.BlockSpec(memory_space=pltpu.VMEM)] * 2,
        out_specs=pl.BlockSpec(memory_space=pltpu.HBM),
        scratch_shapes=[pltpu.VMEM((1024, 512), jnp.float32), pltpu.SemaphoreType.DMA],
        compiler_params=pltpu.CompilerParams(vmem_limit_bytes=16 * 1024 * 1024),
    )(
        pltpu.with_memory_space_constraint(inflated, pltpu.VMEM),
        pltpu.with_memory_space_constraint(totals, pltpu.VMEM),
    )


def solution(mesh):
    spec = P("row", "col")
    return jax.shard_map(local, mesh=mesh, in_specs=(spec, spec, spec), out_specs=spec, check_vma=False)
```

```python
import functools

import jax
import jax.numpy as jnp
from jax import lax
from jax.experimental import pallas as pl
from jax.experimental.pallas import tpu as pltpu
from jax.sharding import PartitionSpec as P

TILE = 256
HALF = 128
MESH = pl.DeviceIdType.MESH
SIDE = 4
SLOTS = 4
STEPS = 3
UP = (0, 2, 0)
DOWN = (2, 0, 2)


def turn(offset, times):
    dx, dz = offset
    for _ in range(times):
        dx, dz = -dz, dx
    return dx, dz


def around(offset, parent, first):
    return [(turn(offset, k), turn(parent, k), first, 2) for k in range(4)]


PHASES = (
    around((1, 0), (0, 0), 0),
    around((1, 0), (0, 0), 2),
    around((1, 1), (1, 0), 0),
    around((1, 1), (1, 0), 2),
    around((2, 1), (1, 1), 0),
    around((2, 1), (1, 1), 2),
    [((2, 0), (1, 0), 0, 2), ((2, 0), (-1, 0), 2, 2), ((0, 2), (0, 1), 0, 2), ((0, 2), (0, -1), 2, 2)],
    [((2, 2), (2, 1), 0, 1), ((2, 2), (2, -1), 1, 1), ((2, 2), (1, 2), 2, 1), ((2, 2), (-1, 2), 3, 1)],
    [((2, 2), (2, 1), 0, 1), ((2, 2), (2, -1), 1, 1), ((2, 2), (1, 2), 2, 1), ((2, 2), (-1, 2), 3, 1)],
)
CODES = {
    1: [leg[:2] for leg in PHASES[1]],
    3: [leg[:2] for leg in PHASES[3]],
    5: [leg[:2] for leg in PHASES[5]],
    6: [((2, 0), (1, 0)), ((0, 2), (0, 1))],
    7: [((2, 2), (2, 1))],
}
MOMENTS = (
    ("a", 0), ("c", 0), ("a", 1), ("b", 1), ("a", 2), ("c", 1), ("a", 3), ("b", 2),
    ("a", 4), ("c", 2), ("a", 5), ("b", 3), ("c", 3), ("a", 6), ("a", 7), ("a", 8),
)


def compute_plan():
    when = {moment: i for i, moment in enumerate(MOMENTS)}
    arrive = {(0, 0): 0}
    for number, legs in enumerate(PHASES):
        for (dx, dz), _, _, _ in legs:
            arrive[dx % SIDE, dz % SIDE] = when["a", number]
    orders, ready = {}, {}
    for delta in range(SIDE):
        for parity in range(2):
            able = {}
            for (dx, dz), moment in arrive.items():
                dy = (delta - dz) % SIDE
                quarter = (parity + dx) % 2
                step = {0: 0, 2: 3, 3: 1 + quarter, 1: 2 - quarter}[dy]
                able[dx, dz] = max(moment, when["c", step])
            order = sorted(able, key=lambda o: (able[o], o))
            orders[delta, parity] = order
            ready[delta, parity] = [able[o] for o in order]
    counts, done = [], 0
    for i in range(len(MOMENTS)):
        take = min(sum(1 for w in ready[v] if w <= i) for v in ready) - done
        counts.append(take)
        done += take
    assert done == SIDE * SIDE and counts[-1] == 1
    return orders, counts


ORDERS, COUNTS = compute_plan()


def kernel(
    pattern_ref, weights_ref, panel_ref, total, sums_ref,
    own, left, graph, panel, pattern, meta, part, parts, local_sem,
    a_send, a_recv, b_send, b_recv, c_send, c_recv, m_send, m_recv, t_send, t_recv, both,
):
    row, col = lax.axis_index("row"), lax.axis_index("col")
    y, core = row // 2, row % 2
    z, x = col // SIDE, col % SIDE

    def wrap(v):
        return (v + 2 * SIDE) % SIDE

    def at(dx, dz):
        return wrap(z + dz) * SIDE + wrap(x + dx)

    def lane(dy):
        return wrap(y + dy) * 2 + core

    def lane_of(dy, which):
        return wrap(y + dy) * 2 + which

    other = y * 2 + 1 - core

    load_p = pltpu.make_async_copy(pattern_ref, pattern, local_sem.at[1])
    mine = pl.multiple_of(row * 4, 4)
    load_b = pltpu.make_async_copy(panel_ref, panel.at[pl.ds(mine, 4)], local_sem.at[2])
    load_p.start()
    def load_a(i, first, size):
        rows = pl.ds(first, size)
        return pltpu.make_async_copy(weights_ref.at[rows], own.at[rows], local_sem.at[i])

    load_a(0, 512, 512).start()
    load_a(3, 0, 256).start()
    load_a(4, 256, 256).start()

    barrier = pltpu.get_barrier_semaphore()
    for sign in (1, -1):
        for peer in (
            (lane_of(0, 0), at(sign, 0)), (lane_of(0, 1), at(0, sign)), (lane(sign), col),
        ):
            pl.semaphore_signal(barrier, inc=1, device_id=peer, device_id_type=MESH)
    pl.semaphore_signal(barrier, inc=1, device_id=(other, col), device_id_type=MESH)

    load_p.wait()
    bits = [pattern[i % 2, i // 2] for i in range(8)]
    meta[col, 0] = functools.reduce(lambda a, b: a + b, [bits[i] << i for i in range(8)])
    def places(have):
        gaps, extras = [jnp.int32(0)], [jnp.int32(0)]
        for i in range(3):
            gaps.append(gaps[-1] + 1 - have[i])
            extras.append(extras[-1] + have[4 + i])
        return [[(have[s] == 0) & (have[4 + i] == 1) & (gaps[s] == extras[i]) for i in range(4)] for s in range(SLOTS)]

    holds = places(bits)

    def pack(s):
        def tile(i):
            r, c = i // 2 * TILE, i % 2 * TILE
            return own[r:r + TILE, c:c + TILE]

        packed = tile(s)
        for i in range(4):
            packed = jnp.where(holds[s][i], tile(4 + i), packed)
        graph[col, s] = packed

    def remote(source, target, send_sem, recv_sem, device):
        return pltpu.make_async_remote_copy(
            src_ref=source, dst_ref=target, send_sem=send_sem, recv_sem=recv_sem,
            device_id=device, device_id_type=MESH)

    def arrived(block, recv_sem):
        remote(block, block, recv_sem, recv_sem, (row, col)).wait_recv()

    def sent(block, send_sem):
        remote(block, block, send_sem, send_sem, (row, col)).wait_send()

    def send(number):
        for (dx, dz), (px, pz), first, count in PHASES[number]:
            tiles = graph.at[at(-px, -pz), pl.ds(first, count)]
            if number >= 7:
                tiles = tiles.at[:, pl.ds((number - 7) * HALF, HALF)]
            remote(tiles, tiles, a_send, a_recv.at[number], (row, at(dx - px, dz - pz))).start()

    def send_codes(number):
        for (dx, dz), (px, pz) in CODES[number]:
            code = meta.at[at(-px, -pz)]
            remote(code, code, m_send, m_recv.at[number], (row, at(dx - px, dz - pz))).start()

    def a_wait(number):
        if number >= 7:
            arrived(graph.at[0, pl.ds(0, 2)], a_recv.at[number])
        else:
            arrived(graph.at[pl.ds(0, 2)], a_recv.at[number])
        if number in CODES:
            arrived(meta.at[pl.ds(0, len(CODES[number]))], m_recv.at[number])

    def two(device_row, j):
        return panel.at[pl.ds(device_row * 4 + j, 2)]

    def b_copy(way, step):
        pieces = two(lane(-way if step == STEPS else 0), (UP if way > 0 else DOWN)[step - 1])
        return remote(pieces, pieces, b_send, b_recv.at[step - 1], (lane(way), col))

    def b_wait(step):
        arrived(panel.at[pl.ds(0, 4)], b_recv.at[step - 1])

    def c_copy(step, way):
        if step == 0:
            pieces = panel.at[pl.ds(mine, 4)]
        else:
            hops = 2 if step == STEPS else 1
            pieces = two(lane(-way * hops), (UP if way > 0 else DOWN)[step - 1])
        return remote(pieces, pieces, c_send, c_recv.at[step], (other, col))

    def c_wait(step):
        arrived(panel.at[pl.ds(0, 4)], c_recv.at[step])

    def ordered(place):
        index = jnp.int32(0)
        variant = wrap(z - y) * 2 + x % 2
        for v in range(8):
            dx, dz = ORDERS[v // 2, v % 2][place]
            index = jnp.where(variant == v, at(-dx, -dz), index)
        return index

    def unpacked(source, have, holding, i, start, size):
        tile = jnp.zeros((size, TILE), jnp.bfloat16)
        for s in range(SLOTS) if i >= 4 else (i,):
            taken = holding[s][i - 4] if i >= 4 else have[i] == 1
            tile = jnp.where(taken, graph[source, s, start:start + size, :], tile)
        return tile

    def product(source, have, holding, r):
        piece = pl.multiple_of(source * 2, 2)
        return sum(
            jnp.dot(unpacked(source, have, holding, 2 * r + c, 0, TILE), panel[piece + c],
                    preferred_element_type=jnp.float32)
            for c in range(2))

    def code(source):
        present = meta[source, 0]
        have = [(present >> i) & 1 for i in range(8)]
        return have, places(have)

    def add_source(source, first):
        have, holding = code(source)
        for r in range(4):
            rows = pl.ds(r * TILE, TILE)
            value = product(source, have, holding, r)
            if first:
                total[rows, :] = value
            else:
                total[rows, :] += value

    def finish(source, half):
        have, holding = code(source)
        for r in range(4):
            for c in range(2):
                left[r * HALF:(r + 1) * HALF, c * TILE:(c + 1) * TILE] = unpacked(
                    source, have, holding, 2 * r + c, half * HALF, HALF)
        piece = pl.multiple_of(source * 2, 2)
        right = panel[pl.ds(piece, 2)].reshape(2 * TILE, 512)
        value = jnp.dot(left[...], right, preferred_element_type=jnp.float32)
        sums = jnp.zeros((8, 512), jnp.float32)
        for r in range(4):
            rows = pl.ds(r * TILE + half * HALF, HALF)
            square = total[rows, :] + value[r * HALF:(r + 1) * HALF]
            square = square * square
            total[rows, :] = square
            sums += jnp.sum(square.reshape(HALF // 8, 8, 512), axis=0)
        return sums

    def own_pair(number, along):
        for sign in (1, -1):
            tiles = graph.at[col, pl.ds(2 * number, 2)]
            target = at(sign * (1 - along), sign * along)
            remote(tiles, tiles, a_send, a_recv.at[number], (row, target)).start()

    load_a(0, 512, 512).wait()
    load_a(3, 0, 256).wait()
    pack(0)
    pack(1)
    load_b.start()
    pl.semaphore_wait(barrier, 7)
    pl.semaphore_signal(both, inc=1, device_id=(other, col), device_id_type=MESH)
    own_pair(0, core)
    load_a(4, 256, 256).wait()
    pack(2)
    pack(3)
    pl.semaphore_wait(both, 1)
    own_pair(0, 1 - core)
    own_pair(1, core)
    own_pair(1, 1 - core)
    send_codes(1)
    load_b.wait()
    for step in (1, 2):
        for way in (1, -1):
            b_copy(way, step).start()
    c_copy(0, 1).start()

    done = 0
    sums = []
    for (kind, number), count in zip(MOMENTS, COUNTS):
        if kind == "a":
            a_wait(number)
            for later in {0: (2,), 1: (3,), 2: (4,), 3: (5, 6), 5: (7, 8)}.get(number, ()):
                send(later)
                if later in CODES:
                    send_codes(later)
        elif kind == "b":
            b_wait(number)
            for way in (1, -1):
                c_copy(number, way).start()
            if number + 2 <= STEPS:
                for way in (1, -1):
                    b_copy(way, number + 2).start()
        else:
            c_wait(number)
        for _ in range(count):
            if done < SIDE * SIDE - 1:
                add_source(ordered(done), done == 0)
            done += 1
        if kind == "a" and number >= 7:
            sums.append(finish(ordered(SIDE * SIDE - 1), number - 7))

    sums = jnp.sum(sums[0] + sums[1], axis=0, keepdims=True)
    part[...] = sums
    for i in range(1, 8):
        remote(part, parts.at[row], t_send, t_recv, ((row + i) % 8, col)).start()
    parts[row] = sums

    sent(graph.at[pl.ds(0, 15)], a_send)
    sent(meta.at[pl.ds(0, 15)], m_send)
    sent(panel.at[pl.ds(0, 4 * STEPS)], b_send)
    sent(panel.at[pl.ds(0, 4 + 4 * STEPS)], c_send)

    arrived(parts.at[pl.ds(0, 7)], t_recv)
    whole = parts[0]
    for i in range(1, 8):
        whole += parts[i]
    sums_ref[...] = whole
    sent(parts.at[pl.ds(0, 7)], t_send)


def divide(inflated_ref, totals_ref, flow_ref, held, sem):
    size = 1024 // 8
    for i in range(8):
        rows = pl.ds(i * size, size)
        held[rows, :] = jnp.float32(8192) * inflated_ref[rows, :] / totals_ref[...]
        pltpu.make_async_copy(held.at[rows], flow_ref.at[rows], sem).start()
    pltpu.make_async_copy(held, flow_ref, sem).wait()


def local(weights, panel, pattern):
    def stay(array):
        return pltpu.with_memory_space_constraint(array, pltpu.HBM)

    inflated, totals = pl.pallas_call(
        kernel,
        out_shape=(
            pltpu.VMEM((1024, 512), jnp.float32),
            pltpu.VMEM((1, 512), jnp.float32),
        ),
        in_specs=[pl.BlockSpec(memory_space=pltpu.HBM)] * 3,
        out_specs=(
            pl.BlockSpec(memory_space=pltpu.VMEM),
            pl.BlockSpec(memory_space=pltpu.VMEM),
        ),
        scratch_shapes=[
            pltpu.VMEM((1024, 512), jnp.bfloat16),
            pltpu.VMEM((4 * HALF, 2 * TILE), jnp.bfloat16),
            pltpu.VMEM((16, SLOTS, TILE, TILE), jnp.bfloat16),
            pltpu.VMEM((32, TILE, 512), jnp.bfloat16),
            pltpu.SMEM((2, 4), jnp.int32),
            pltpu.SMEM((16, 128), jnp.int32),
            pltpu.VMEM((1, 512), jnp.float32),
            pltpu.VMEM((8, 1, 512), jnp.float32),
            pltpu.SemaphoreType.DMA((5,)),
            pltpu.SemaphoreType.DMA,
            pltpu.SemaphoreType.DMA((len(PHASES),)),
            pltpu.SemaphoreType.DMA,
            pltpu.SemaphoreType.DMA((STEPS,)),
            pltpu.SemaphoreType.DMA,
            pltpu.SemaphoreType.DMA((STEPS + 1,)),
            pltpu.SemaphoreType.DMA,
            pltpu.SemaphoreType.DMA((len(PHASES),)),
            pltpu.SemaphoreType.DMA,
            pltpu.SemaphoreType.DMA,
            pltpu.SemaphoreType.REGULAR,
        ],
        compiler_params=pltpu.CompilerParams(
            collective_id=0, has_side_effects=True, vmem_limit_bytes=40 * 1024 * 1024
        ),
        cost_estimate=pl.CostEstimate(
            flops=2 * 1024 * 8192 * 512, bytes_accessed=4 * 1024 * 1024, transcendentals=0
        ),
    )(stay(pattern.T), stay(weights), stay(panel.reshape(4, TILE, 512)))
    return pl.pallas_call(
        divide,
        out_shape=jax.ShapeDtypeStruct((1024, 512), jnp.float32),
        in_specs=[pl.BlockSpec(memory_space=pltpu.VMEM)] * 2,
        out_specs=pl.BlockSpec(memory_space=pltpu.HBM),
        scratch_shapes=[pltpu.VMEM((1024, 512), jnp.float32), pltpu.SemaphoreType.DMA],
        compiler_params=pltpu.CompilerParams(vmem_limit_bytes=16 * 1024 * 1024),
    )(
        pltpu.with_memory_space_constraint(inflated, pltpu.VMEM),
        pltpu.with_memory_space_constraint(totals, pltpu.VMEM),
    )


def solution(mesh):
    spec = P("row", "col")
    return jax.shard_map(local, mesh=mesh, in_specs=(spec, spec, spec), out_specs=spec, check_vma=False)
```

```python
import functools

import jax
import jax.numpy as jnp
from jax import lax
from jax.experimental import pallas as pl
from jax.experimental.pallas import tpu as pltpu
from jax.sharding import PartitionSpec as P

TILE = 256
CUTS = ((0, 192), (192, 64))
MESH = pl.DeviceIdType.MESH
SIDE = 4
SLOTS = 4
STEPS = 3
UP = (0, 2, 0)
DOWN = (2, 0, 2)


def turn(offset, times):
    dx, dz = offset
    for _ in range(times):
        dx, dz = -dz, dx
    return dx, dz


def around(offset, parent, first):
    return [(turn(offset, k), turn(parent, k), first, 2) for k in range(4)]


PHASES = (
    around((1, 0), (0, 0), 0),
    around((1, 0), (0, 0), 2),
    around((1, 1), (1, 0), 0),
    around((1, 1), (1, 0), 2),
    around((2, 1), (1, 1), 0),
    around((2, 1), (1, 1), 2),
    [((2, 0), (1, 0), 0, 2), ((2, 0), (-1, 0), 2, 2), ((0, 2), (0, 1), 0, 2), ((0, 2), (0, -1), 2, 2)],
    [((2, 2), (2, 1), 0, 1), ((2, 2), (2, -1), 1, 1), ((2, 2), (1, 2), 2, 1), ((2, 2), (-1, 2), 3, 1)],
    [((2, 2), (2, 1), 0, 1), ((2, 2), (2, -1), 1, 1), ((2, 2), (1, 2), 2, 1), ((2, 2), (-1, 2), 3, 1)],
)
CODES = {
    1: [leg[:2] for leg in PHASES[1]],
    3: [leg[:2] for leg in PHASES[3]],
    5: [leg[:2] for leg in PHASES[5]],
    6: [((2, 0), (1, 0)), ((0, 2), (0, 1))],
    7: [((2, 2), (2, 1))],
}
MOMENTS = (
    ("a", 0), ("c", 0), ("a", 1), ("b", 1), ("a", 2), ("c", 1), ("a", 3), ("b", 2),
    ("a", 4), ("c", 2), ("a", 5), ("b", 3), ("c", 3), ("a", 6), ("a", 7), ("a", 8),
)


def compute_plan():
    when = {moment: i for i, moment in enumerate(MOMENTS)}
    arrive = {(0, 0): 0}
    for number, legs in enumerate(PHASES):
        for (dx, dz), _, _, _ in legs:
            arrive[dx % SIDE, dz % SIDE] = when["a", number]
    orders, ready = {}, {}
    for delta in range(SIDE):
        for parity in range(2):
            able = {}
            for (dx, dz), moment in arrive.items():
                dy = (delta - dz) % SIDE
                quarter = (parity + dx) % 2
                step = {0: 0, 2: 3, 3: 1 + quarter, 1: 2 - quarter}[dy]
                able[dx, dz] = max(moment, when["c", step])
            order = sorted(able, key=lambda o: (able[o], o))
            orders[delta, parity] = order
            ready[delta, parity] = [able[o] for o in order]
    counts, done = [], 0
    for i in range(len(MOMENTS)):
        take = min(sum(1 for w in ready[v] if w <= i) for v in ready) - done
        counts.append(take)
        done += take
    assert done == SIDE * SIDE and counts[-1] == 1
    return orders, counts


ORDERS, COUNTS = compute_plan()


def kernel(
    pattern_ref, weights_ref, panel_ref, total, sums_ref,
    own, left, graph, panel, pattern, meta, codes, part, parts, local_sem,
    a_send, a_recv, b_send, b_recv, c_send, c_recv, m_send, m_recv, t_send, t_recv, both,
):
    row, col = lax.axis_index("row"), lax.axis_index("col")
    y, core = row // 2, row % 2
    z, x = col // SIDE, col % SIDE

    def wrap(v):
        return (v + 2 * SIDE) % SIDE

    def at(dx, dz):
        return wrap(z + dz) * SIDE + wrap(x + dx)

    def lane(dy):
        return wrap(y + dy) * 2 + core

    def lane_of(dy, which):
        return wrap(y + dy) * 2 + which

    other = y * 2 + 1 - core

    load_p = pltpu.make_async_copy(pattern_ref, pattern, local_sem.at[1])
    mine = pl.multiple_of(row * 4, 4)
    load_b = pltpu.make_async_copy(panel_ref, panel.at[pl.ds(mine, 4)], local_sem.at[2])
    load_p.start()
    def load_a(i, first, size):
        rows = pl.ds(first, size)
        return pltpu.make_async_copy(weights_ref.at[rows], own.at[rows], local_sem.at[i])

    load_a(0, 512, 512).start()
    load_a(3, 0, 256).start()
    load_a(4, 256, 256).start()

    barrier = pltpu.get_barrier_semaphore()
    for sign in (1, -1):
        for peer in (
            (lane_of(0, 0), at(sign, 0)), (lane_of(0, 1), at(0, sign)), (lane(sign), col),
        ):
            pl.semaphore_signal(barrier, inc=1, device_id=peer, device_id_type=MESH)
    pl.semaphore_signal(barrier, inc=1, device_id=(other, col), device_id_type=MESH)

    load_p.wait()
    bits = [pattern[i % 2, i // 2] for i in range(8)]
    number = functools.reduce(lambda a, b: a + b, [bits[i] << i for i in range(8)])
    codes[col] = jnp.full((1, 128), number, jnp.int32)
    meta[col] = number
    def places(have):
        gaps, extras = [jnp.int32(0)], [jnp.int32(0)]
        for i in range(3):
            gaps.append(gaps[-1] + 1 - have[i])
            extras.append(extras[-1] + have[4 + i])
        return [[(have[s] == 0) & (have[4 + i] == 1) & (gaps[s] == extras[i]) for i in range(4)] for s in range(SLOTS)]

    holds = places(bits)

    def pack(s):
        def tile(i):
            r, c = i // 2 * TILE, i % 2 * TILE
            return own[r:r + TILE, c:c + TILE]

        packed = tile(s)
        for i in range(4):
            packed = jnp.where(holds[s][i], tile(4 + i), packed)
        graph[col, s] = packed

    def remote(source, target, send_sem, recv_sem, device):
        return pltpu.make_async_remote_copy(
            src_ref=source, dst_ref=target, send_sem=send_sem, recv_sem=recv_sem,
            device_id=device, device_id_type=MESH)

    def arrived(block, recv_sem):
        remote(block, block, recv_sem, recv_sem, (row, col)).wait_recv()

    def sent(block, send_sem):
        remote(block, block, send_sem, send_sem, (row, col)).wait_send()

    def send(number):
        for (dx, dz), (px, pz), first, count in PHASES[number]:
            tiles = graph.at[at(-px, -pz), pl.ds(first, count)]
            if number >= 7:
                tiles = tiles.at[:, pl.ds(*CUTS[number - 7])]
            remote(tiles, tiles, a_send, a_recv.at[number], (row, at(dx - px, dz - pz))).start()

    def send_codes(number):
        for (dx, dz), (px, pz) in CODES[number]:
            code = codes.at[at(-px, -pz)]
            remote(code, code, m_send, m_recv.at[number], (row, at(dx - px, dz - pz))).start()

    def a_wait(number):
        if number >= 7:
            arrived(graph.at[0, :, pl.ds(*CUTS[number - 7])], a_recv.at[number])
        else:
            arrived(graph.at[pl.ds(0, 2)], a_recv.at[number])

    def two(device_row, j):
        return panel.at[pl.ds(device_row * 4 + j, 2)]

    def b_copy(way, step):
        pieces = two(lane(-way if step == STEPS else 0), (UP if way > 0 else DOWN)[step - 1])
        return remote(pieces, pieces, b_send, b_recv.at[step - 1], (lane(way), col))

    def b_wait(step):
        arrived(panel.at[pl.ds(0, 4)], b_recv.at[step - 1])

    def c_copy(step, way):
        if step == 0:
            pieces = panel.at[pl.ds(mine, 4)]
        else:
            hops = 2 if step == STEPS else 1
            pieces = two(lane(-way * hops), (UP if way > 0 else DOWN)[step - 1])
        return remote(pieces, pieces, c_send, c_recv.at[step], (other, col))

    def c_wait(step):
        arrived(panel.at[pl.ds(0, 4)], c_recv.at[step])

    def ordered(place):
        index = jnp.int32(0)
        variant = wrap(z - y) * 2 + x % 2
        for v in range(8):
            dx, dz = ORDERS[v // 2, v % 2][place]
            index = jnp.where(variant == v, at(-dx, -dz), index)
        return index

    def unpacked(source, have, holding, i, start, size):
        tile = jnp.zeros((size, TILE), jnp.bfloat16)
        for s in range(SLOTS) if i >= 4 else (i,):
            taken = holding[s][i - 4] if i >= 4 else have[i] == 1
            tile = jnp.where(taken, graph[source, s, start:start + size, :], tile)
        return tile

    def product(source, have, holding, r):
        piece = pl.multiple_of(source * 2, 2)
        return sum(
            jnp.dot(unpacked(source, have, holding, 2 * r + c, 0, TILE), panel[piece + c],
                    preferred_element_type=jnp.float32)
            for c in range(2))

    def code(source):
        present = meta[source]
        have = [(present >> i) & 1 for i in range(8)]
        return have, places(have)

    def add_source(source, first):
        have, holding = code(source)
        for r in range(4):
            rows = pl.ds(r * TILE, TILE)
            value = product(source, have, holding, r)
            if first:
                total[rows, :] = value
            else:
                total[rows, :] += value

    def finish(source, start, size):
        have, holding = code(source)
        for r in range(4):
            for c in range(2):
                left[r * size:(r + 1) * size, c * TILE:(c + 1) * TILE] = unpacked(
                    source, have, holding, 2 * r + c, start, size)
        piece = pl.multiple_of(source * 2, 2)
        right = panel[pl.ds(piece, 2)].reshape(2 * TILE, 512)
        value = jnp.dot(left[:4 * size], right, preferred_element_type=jnp.float32)
        sums = jnp.zeros((8, 512), jnp.float32)
        for r in range(4):
            rows = pl.ds(r * TILE + start, size)
            square = total[rows, :] + value[r * size:(r + 1) * size]
            square = square * square
            total[rows, :] = square
            sums += jnp.sum(square.reshape(size // 8, 8, 512), axis=0)
        return sums

    def own_pair(number, along):
        for sign in (1, -1):
            tiles = graph.at[col, pl.ds(2 * number, 2)]
            target = at(sign * (1 - along), sign * along)
            remote(tiles, tiles, a_send, a_recv.at[number], (row, target)).start()

    load_a(0, 512, 512).wait()
    load_a(3, 0, 256).wait()
    pack(0)
    pack(1)
    load_b.start()
    pl.semaphore_wait(barrier, 7)
    pl.semaphore_signal(both, inc=1, device_id=(other, col), device_id_type=MESH)
    own_pair(0, core)
    load_a(4, 256, 256).wait()
    pack(2)
    pack(3)
    pl.semaphore_wait(both, 1)
    send_codes(1)
    own_pair(0, 1 - core)
    own_pair(1, core)
    own_pair(1, 1 - core)
    load_b.wait()
    for step in (1, 2):
        for way in (1, -1):
            b_copy(way, step).start()
    c_copy(0, 1).start()

    done = 0
    sums = []
    for (kind, number), count in zip(MOMENTS, COUNTS):
        if kind == "a":
            a_wait(number)
            heard = {0: (1,), 2: (3, 6), 4: (5,), 6: (7,)}.get(number, ())
            for phase in heard:
                arrived(codes.at[pl.ds(0, len(CODES[phase]))], m_recv.at[phase])
            for phase in {0: (3, 6), 2: (5,), 4: (7,)}.get(number, ()):
                send_codes(phase)
            for later in {0: (2,), 1: (3,), 2: (4,), 3: (5,), 4: (6,), 5: (7, 8)}.get(number, ()):
                send(later)
            for phase in heard:
                for (dx, dz), _ in CODES[phase]:
                    source = at(-dx, -dz)
                    meta[source] = jnp.max(codes[source])
        elif kind == "b":
            b_wait(number)
            for way in (1, -1):
                c_copy(number, way).start()
            if number + 2 <= STEPS:
                for way in (1, -1):
                    b_copy(way, number + 2).start()
        else:
            c_wait(number)
        for _ in range(count):
            if done < SIDE * SIDE - 1:
                add_source(ordered(done), done == 0)
            done += 1
        if kind == "a" and number >= 7:
            sums.append(finish(ordered(SIDE * SIDE - 1), *CUTS[number - 7]))

    sums = jnp.sum(sums[0] + sums[1], axis=0, keepdims=True)
    part[...] = sums
    for i in range(1, 8):
        remote(part, parts.at[row], t_send, t_recv, ((row + i) % 8, col)).start()
    parts[row] = sums

    sent(graph.at[pl.ds(0, 15)], a_send)
    sent(codes.at[pl.ds(0, 15)], m_send)
    sent(panel.at[pl.ds(0, 4 * STEPS)], b_send)
    sent(panel.at[pl.ds(0, 4 + 4 * STEPS)], c_send)

    arrived(parts.at[pl.ds(0, 7)], t_recv)
    whole = parts[0]
    for i in range(1, 8):
        whole += parts[i]
    sums_ref[...] = whole
    sent(parts.at[pl.ds(0, 7)], t_send)


def divide(inflated_ref, totals_ref, flow_ref, held, sem):
    size = 1024 // 8
    for i in range(8):
        rows = pl.ds(i * size, size)
        held[rows, :] = jnp.float32(8192) * inflated_ref[rows, :] / totals_ref[...]
        pltpu.make_async_copy(held.at[rows], flow_ref.at[rows], sem).start()
    pltpu.make_async_copy(held, flow_ref, sem).wait()


def local(weights, panel, pattern):
    def stay(array):
        return pltpu.with_memory_space_constraint(array, pltpu.HBM)

    inflated, totals = pl.pallas_call(
        kernel,
        out_shape=(
            pltpu.VMEM((1024, 512), jnp.float32),
            pltpu.VMEM((1, 512), jnp.float32),
        ),
        in_specs=[pl.BlockSpec(memory_space=pltpu.HBM)] * 3,
        out_specs=(
            pl.BlockSpec(memory_space=pltpu.VMEM),
            pl.BlockSpec(memory_space=pltpu.VMEM),
        ),
        scratch_shapes=[
            pltpu.VMEM((1024, 512), jnp.bfloat16),
            pltpu.VMEM((4 * CUTS[0][1], 2 * TILE), jnp.bfloat16),
            pltpu.VMEM((16, SLOTS, TILE, TILE), jnp.bfloat16),
            pltpu.VMEM((32, TILE, 512), jnp.bfloat16),
            pltpu.SMEM((2, 4), jnp.int32),
            pltpu.SMEM((16,), jnp.int32),
            pltpu.VMEM((16, 1, 128), jnp.int32),
            pltpu.VMEM((1, 512), jnp.float32),
            pltpu.VMEM((8, 1, 512), jnp.float32),
            pltpu.SemaphoreType.DMA((5,)),
            pltpu.SemaphoreType.DMA,
            pltpu.SemaphoreType.DMA((len(PHASES),)),
            pltpu.SemaphoreType.DMA,
            pltpu.SemaphoreType.DMA((STEPS,)),
            pltpu.SemaphoreType.DMA,
            pltpu.SemaphoreType.DMA((STEPS + 1,)),
            pltpu.SemaphoreType.DMA,
            pltpu.SemaphoreType.DMA((len(PHASES),)),
            pltpu.SemaphoreType.DMA,
            pltpu.SemaphoreType.DMA,
            pltpu.SemaphoreType.REGULAR,
        ],
        compiler_params=pltpu.CompilerParams(
            collective_id=0, has_side_effects=True, vmem_limit_bytes=40 * 1024 * 1024
        ),
        cost_estimate=pl.CostEstimate(
            flops=2 * 1024 * 8192 * 512, bytes_accessed=4 * 1024 * 1024, transcendentals=0
        ),
    )(stay(pattern.T), stay(weights), stay(panel.reshape(4, TILE, 512)))
    return pl.pallas_call(
        divide,
        out_shape=jax.ShapeDtypeStruct((1024, 512), jnp.float32),
        in_specs=[pl.BlockSpec(memory_space=pltpu.VMEM)] * 2,
        out_specs=pl.BlockSpec(memory_space=pltpu.HBM),
        scratch_shapes=[pltpu.VMEM((1024, 512), jnp.float32), pltpu.SemaphoreType.DMA],
        compiler_params=pltpu.CompilerParams(vmem_limit_bytes=16 * 1024 * 1024),
    )(
        pltpu.with_memory_space_constraint(inflated, pltpu.VMEM),
        pltpu.with_memory_space_constraint(totals, pltpu.VMEM),
    )


def solution(mesh):
    spec = P("row", "col")
    return jax.shard_map(local, mesh=mesh, in_specs=(spec, spec, spec), out_specs=spec, check_vma=False)
```

```python
import functools

import jax
import jax.numpy as jnp
from jax import lax
from jax.experimental import pallas as pl
from jax.experimental.pallas import tpu as pltpu
from jax.sharding import PartitionSpec as P

TILE = 256
CUTS = ((0, 192), (192, 64))
MESH = pl.DeviceIdType.MESH
SIDE = 4
SLOTS = 4
STEPS = 3
UP = (0, 2, 0)
DOWN = (2, 0, 2)


def turn(offset, times):
    dx, dz = offset
    for _ in range(times):
        dx, dz = -dz, dx
    return dx, dz


def around(offset, parent, first):
    return [(turn(offset, k), turn(parent, k), first, 2) for k in range(4)]


PHASES = (
    around((1, 0), (0, 0), 0),
    around((1, 0), (0, 0), 2),
    around((1, 1), (1, 0), 0),
    around((1, 1), (1, 0), 2),
    around((2, 1), (1, 1), 0),
    around((2, 1), (1, 1), 2),
    [((2, 0), (1, 0), 0, 2), ((2, 0), (-1, 0), 2, 2), ((0, 2), (0, 1), 0, 2), ((0, 2), (0, -1), 2, 2)],
    [((2, 2), (2, 1), 0, 1), ((2, 2), (2, -1), 1, 1), ((2, 2), (1, 2), 2, 1), ((2, 2), (-1, 2), 3, 1)],
    [((2, 2), (2, 1), 0, 1), ((2, 2), (2, -1), 1, 1), ((2, 2), (1, 2), 2, 1), ((2, 2), (-1, 2), 3, 1)],
)
CODES = {
    1: [leg[:2] for leg in PHASES[1]],
    3: [leg[:2] for leg in PHASES[3]],
    5: [leg[:2] for leg in PHASES[5]],
    6: [((2, 0), (1, 0)), ((0, 2), (0, 1))],
    7: [((2, 2), (2, 1))],
}
MOMENTS = (
    ("a", 0), ("c", 0), ("a", 1), ("b", 1), ("a", 2), ("c", 1), ("a", 3), ("b", 2),
    ("a", 4), ("c", 2), ("a", 5), ("b", 3), ("c", 3), ("a", 6), ("a", 7), ("a", 8),
)


def compute_plan():
    when = {moment: i for i, moment in enumerate(MOMENTS)}
    arrive = {(0, 0): 0}
    for number, legs in enumerate(PHASES):
        for (dx, dz), _, _, _ in legs:
            arrive[dx % SIDE, dz % SIDE] = when["a", number]
    orders, ready = {}, {}
    for delta in range(SIDE):
        for parity in range(2):
            able = {}
            for (dx, dz), moment in arrive.items():
                dy = (delta - dz) % SIDE
                quarter = (parity + dx) % 2
                step = {0: 0, 2: 3, 3: 1 + quarter, 1: 2 - quarter}[dy]
                able[dx, dz] = max(moment, when["c", step])
            order = sorted(able, key=lambda o: (able[o], o))
            orders[delta, parity] = order
            ready[delta, parity] = [able[o] for o in order]
    counts, done = [], 0
    for i in range(len(MOMENTS)):
        take = min(sum(1 for w in ready[v] if w <= i) for v in ready) - done
        counts.append(take)
        done += take
    assert done == SIDE * SIDE and counts[-1] == 1
    return orders, counts


ORDERS, COUNTS = compute_plan()


def kernel(
    pattern_ref, weights_ref, panel_ref, total, sums_ref,
    own, left, graph, panel, pattern, meta, codes, part, parts, local_sem,
    a_send, a_recv, b_send, b_recv, c_send, c_recv, m_send, m_recv, t_send, t_recv, both,
):
    row, col = lax.axis_index("row"), lax.axis_index("col")
    y, core = row // 2, row % 2
    z, x = col // SIDE, col % SIDE

    def wrap(v):
        return (v + 2 * SIDE) % SIDE

    def at(dx, dz):
        return wrap(z + dz) * SIDE + wrap(x + dx)

    def lane(dy):
        return wrap(y + dy) * 2 + core

    def lane_of(dy, which):
        return wrap(y + dy) * 2 + which

    other = y * 2 + 1 - core

    load_p = pltpu.make_async_copy(pattern_ref, pattern, local_sem.at[1])
    mine = pl.multiple_of(row * 4, 4)
    load_b = pltpu.make_async_copy(panel_ref, panel.at[pl.ds(mine, 4)], local_sem.at[2])
    load_p.start()
    def load_a(i, first, size):
        rows = pl.ds(first, size)
        return pltpu.make_async_copy(weights_ref.at[rows], own.at[rows], local_sem.at[i])

    load_a(0, 512, 512).start()
    load_a(3, 0, 256).start()
    load_a(4, 256, 256).start()

    barrier = pltpu.get_barrier_semaphore()
    for sign in (1, -1):
        for peer in (
            (lane_of(0, 0), at(sign, 0)), (lane_of(0, 1), at(0, sign)), (lane(sign), col),
        ):
            pl.semaphore_signal(barrier, inc=1, device_id=peer, device_id_type=MESH)
    pl.semaphore_signal(barrier, inc=1, device_id=(other, col), device_id_type=MESH)

    load_p.wait()
    bits = [pattern[i % 2, i // 2] for i in range(8)]
    number = functools.reduce(lambda a, b: a + b, [bits[i] << i for i in range(8)])
    codes[col] = jnp.full((1, 128), number, jnp.int32)
    meta[col] = number
    def places(have):
        gaps, extras = [jnp.int32(0)], [jnp.int32(0)]
        for i in range(3):
            gaps.append(gaps[-1] + 1 - have[i])
            extras.append(extras[-1] + have[4 + i])
        return [[(have[s] == 0) & (have[4 + i] == 1) & (gaps[s] == extras[i]) for i in range(4)] for s in range(SLOTS)]

    holds = places(bits)

    def pack(s):
        def tile(i):
            r, c = i // 2 * TILE, i % 2 * TILE
            return own[r:r + TILE, c:c + TILE]

        packed = tile(s)
        for i in range(4):
            packed = jnp.where(holds[s][i], tile(4 + i), packed)
        graph[col, s] = packed

    def remote(source, target, send_sem, recv_sem, device):
        return pltpu.make_async_remote_copy(
            src_ref=source, dst_ref=target, send_sem=send_sem, recv_sem=recv_sem,
            device_id=device, device_id_type=MESH)

    def arrived(block, recv_sem):
        remote(block, block, recv_sem, recv_sem, (row, col)).wait_recv()

    def sent(block, send_sem):
        remote(block, block, send_sem, send_sem, (row, col)).wait_send()

    def send(number):
        for (dx, dz), (px, pz), first, count in PHASES[number]:
            tiles = graph.at[at(-px, -pz), pl.ds(first, count)]
            if number >= 7:
                tiles = tiles.at[:, pl.ds(*CUTS[number - 7])]
            remote(tiles, tiles, a_send, a_recv.at[number], (row, at(dx - px, dz - pz))).start()

    def send_codes(number):
        for (dx, dz), (px, pz) in CODES[number]:
            code = codes.at[at(-px, -pz)]
            remote(code, code, m_send, m_recv.at[number], (row, at(dx - px, dz - pz))).start()

    def a_wait(number):
        if number >= 7:
            arrived(graph.at[0, :, pl.ds(*CUTS[number - 7])], a_recv.at[number])
        else:
            arrived(graph.at[pl.ds(0, 2)], a_recv.at[number])

    def two(device_row, j):
        return panel.at[pl.ds(device_row * 4 + j, 2)]

    def b_copy(way, step):
        pieces = two(lane(-way if step == STEPS else 0), (UP if way > 0 else DOWN)[step - 1])
        return remote(pieces, pieces, b_send, b_recv.at[step - 1], (lane(way), col))

    def b_wait(step):
        arrived(panel.at[pl.ds(0, 4)], b_recv.at[step - 1])

    def c_copy(step, way):
        if step == 0:
            pieces = panel.at[pl.ds(mine, 4)]
        else:
            hops = 2 if step == STEPS else 1
            pieces = two(lane(-way * hops), (UP if way > 0 else DOWN)[step - 1])
        return remote(pieces, pieces, c_send, c_recv.at[step], (other, col))

    def c_wait(step):
        arrived(panel.at[pl.ds(0, 4)], c_recv.at[step])

    def ordered(place):
        index = jnp.int32(0)
        variant = wrap(z - y) * 2 + x % 2
        for v in range(8):
            dx, dz = ORDERS[v // 2, v % 2][place]
            index = jnp.where(variant == v, at(-dx, -dz), index)
        return index

    def unpacked(source, have, holding, i, start, size):
        tile = jnp.zeros((size, TILE), jnp.bfloat16)
        for s in range(SLOTS) if i >= 4 else (i,):
            taken = holding[s][i - 4] if i >= 4 else have[i] == 1
            tile = jnp.where(taken, graph[source, s, start:start + size, :], tile)
        return tile

    def product(source, have, holding, r):
        piece = pl.multiple_of(source * 2, 2)
        return sum(
            jnp.dot(unpacked(source, have, holding, 2 * r + c, 0, TILE), panel[piece + c],
                    preferred_element_type=jnp.float32)
            for c in range(2))

    def code(source):
        present = meta[source]
        have = [(present >> i) & 1 for i in range(8)]
        return have, places(have)

    def add_source(source, first):
        have, holding = code(source)
        for r in range(4):
            rows = pl.ds(r * TILE, TILE)
            value = product(source, have, holding, r)
            if first:
                total[rows, :] = value
            else:
                total[rows, :] += value

    def finish(source, start, size):
        have, holding = code(source)
        for r in range(4):
            for c in range(2):
                left[r * size:(r + 1) * size, c * TILE:(c + 1) * TILE] = unpacked(
                    source, have, holding, 2 * r + c, start, size)
        piece = pl.multiple_of(source * 2, 2)
        right = panel[pl.ds(piece, 2)].reshape(2 * TILE, 512)
        value = jnp.dot(left[:4 * size], right, preferred_element_type=jnp.float32)
        sums = jnp.zeros((8, 512), jnp.float32)
        for r in range(4):
            rows = pl.ds(r * TILE + start, size)
            square = total[rows, :] + value[r * size:(r + 1) * size]
            square = square * square
            total[rows, :] = square
            sums += jnp.sum(square.reshape(size // 8, 8, 512), axis=0)
        return sums

    def own_pair(number, along):
        for sign in (1, -1):
            tiles = graph.at[col, pl.ds(2 * number, 2)]
            target = at(sign * (1 - along), sign * along)
            remote(tiles, tiles, a_send, a_recv.at[number], (row, target)).start()

    load_a(0, 512, 512).wait()
    load_a(3, 0, 256).wait()
    pack(0)
    pack(1)
    load_b.start()
    pl.semaphore_wait(barrier, 7)
    pl.semaphore_signal(both, inc=1, device_id=(other, col), device_id_type=MESH)
    own_pair(0, core)
    load_a(4, 256, 256).wait()
    pack(2)
    pack(3)
    pl.semaphore_wait(both, 1)
    send_codes(1)
    own_pair(0, 1 - core)
    own_pair(1, core)
    own_pair(1, 1 - core)
    load_b.wait()
    for step in (1, 2):
        for way in (1, -1):
            b_copy(way, step).start()
    c_copy(0, 1).start()

    done = 0
    sums = []
    for (kind, number), count in zip(MOMENTS, COUNTS):
        if kind == "a":
            a_wait(number)
            heard = {0: (1,), 2: (3, 6), 4: (5,), 6: (7,)}.get(number, ())
            for phase in heard:
                arrived(codes.at[pl.ds(0, len(CODES[phase]))], m_recv.at[phase])
            for phase in {0: (3, 6), 2: (5,), 4: (7,)}.get(number, ()):
                send_codes(phase)
            for later in {0: (2,), 1: (3,), 2: (4,), 3: (5,), 4: (6,), 5: (7, 8)}.get(number, ()):
                send(later)
            for phase in heard:
                for (dx, dz), _ in CODES[phase]:
                    source = at(-dx, -dz)
                    meta[source] = jnp.max(codes[source])
        elif kind == "b":
            b_wait(number)
            for way in (1, -1):
                c_copy(number, way).start()
            if number + 2 <= STEPS:
                for way in (1, -1):
                    b_copy(way, number + 2).start()
        else:
            c_wait(number)
        for _ in range(count):
            if done < SIDE * SIDE - 1:
                add_source(ordered(done), done == 0)
            done += 1
        if kind == "a" and number >= 7:
            sums.append(finish(ordered(SIDE * SIDE - 1), *CUTS[number - 7]))

    sums = jnp.sum(sums[0] + sums[1], axis=0, keepdims=True)
    part[...] = sums
    for i in (4, 3, 5, 2, 6, 7, 1):
        remote(part, parts.at[row], t_send, t_recv, ((row + i) % 8, col)).start()
    parts[row] = sums

    sent(graph.at[pl.ds(0, 15)], a_send)
    sent(codes.at[pl.ds(0, 15)], m_send)
    sent(panel.at[pl.ds(0, 4 * STEPS)], b_send)
    sent(panel.at[pl.ds(0, 4 + 4 * STEPS)], c_send)

    arrived(parts.at[pl.ds(0, 7)], t_recv)
    whole = parts[0]
    for i in range(1, 8):
        whole += parts[i]
    sums_ref[...] = whole
    sent(parts.at[pl.ds(0, 7)], t_send)


def divide(inflated_ref, totals_ref, flow_ref, held, sem):
    size = 1024 // 8
    for i in range(8):
        rows = pl.ds(i * size, size)
        held[rows, :] = jnp.float32(8192) * inflated_ref[rows, :] / totals_ref[...]
        pltpu.make_async_copy(held.at[rows], flow_ref.at[rows], sem).start()
    pltpu.make_async_copy(held, flow_ref, sem).wait()


def local(weights, panel, pattern):
    def stay(array):
        return pltpu.with_memory_space_constraint(array, pltpu.HBM)

    inflated, totals = pl.pallas_call(
        kernel,
        out_shape=(
            pltpu.VMEM((1024, 512), jnp.float32),
            pltpu.VMEM((1, 512), jnp.float32),
        ),
        in_specs=[pl.BlockSpec(memory_space=pltpu.HBM)] * 3,
        out_specs=(
            pl.BlockSpec(memory_space=pltpu.VMEM),
            pl.BlockSpec(memory_space=pltpu.VMEM),
        ),
        scratch_shapes=[
            pltpu.VMEM((1024, 512), jnp.bfloat16),
            pltpu.VMEM((4 * CUTS[0][1], 2 * TILE), jnp.bfloat16),
            pltpu.VMEM((16, SLOTS, TILE, TILE), jnp.bfloat16),
            pltpu.VMEM((32, TILE, 512), jnp.bfloat16),
            pltpu.SMEM((2, 4), jnp.int32),
            pltpu.SMEM((16,), jnp.int32),
            pltpu.VMEM((16, 1, 128), jnp.int32),
            pltpu.VMEM((1, 512), jnp.float32),
            pltpu.VMEM((8, 1, 512), jnp.float32),
            pltpu.SemaphoreType.DMA((5,)),
            pltpu.SemaphoreType.DMA,
            pltpu.SemaphoreType.DMA((len(PHASES),)),
            pltpu.SemaphoreType.DMA,
            pltpu.SemaphoreType.DMA((STEPS,)),
            pltpu.SemaphoreType.DMA,
            pltpu.SemaphoreType.DMA((STEPS + 1,)),
            pltpu.SemaphoreType.DMA,
            pltpu.SemaphoreType.DMA((len(PHASES),)),
            pltpu.SemaphoreType.DMA,
            pltpu.SemaphoreType.DMA,
            pltpu.SemaphoreType.REGULAR,
        ],
        compiler_params=pltpu.CompilerParams(
            collective_id=0, has_side_effects=True, vmem_limit_bytes=40 * 1024 * 1024
        ),
        cost_estimate=pl.CostEstimate(
            flops=2 * 1024 * 8192 * 512, bytes_accessed=4 * 1024 * 1024, transcendentals=0
        ),
    )(stay(pattern.T), stay(weights), stay(panel.reshape(4, TILE, 512)))
    return pl.pallas_call(
        divide,
        out_shape=jax.ShapeDtypeStruct((1024, 512), jnp.float32),
        in_specs=[pl.BlockSpec(memory_space=pltpu.VMEM)] * 2,
        out_specs=pl.BlockSpec(memory_space=pltpu.HBM),
        scratch_shapes=[pltpu.VMEM((1024, 512), jnp.float32), pltpu.SemaphoreType.DMA],
        compiler_params=pltpu.CompilerParams(vmem_limit_bytes=16 * 1024 * 1024),
    )(
        pltpu.with_memory_space_constraint(inflated, pltpu.VMEM),
        pltpu.with_memory_space_constraint(totals, pltpu.VMEM),
    )


def solution(mesh):
    spec = P("row", "col")
    return jax.shard_map(local, mesh=mesh, in_specs=(spec, spec, spec), out_specs=spec, check_vma=False)
```
